32 devices in a mesh: dp: 2 (over y), ctx: 16 (over z, x, core).
Axes of the slice: x: 2, y: 2, z: 4, core: 2. Of those that a mesh axis runs over, the one named last changes fastest.
Arguments:
- base_ids: int32 [8192], P(('dp', 'ctx')), parts along dimension 0, may hold values from 0 to 4
- complement: int32 [5], replicated, may hold values from 0 to 4, each once
- embedding: bfloat16 [5, 768], replicated, may hold values from -6 to 6
- w_gate: bfloat16 [768, 768], replicated, may hold values from -0.21875 to 0.21875
- w_mix: bfloat16 [768, 1024], replicated, may hold values from -0.21875 to 0.21875
- w_step: bfloat16 [768, 12], replicated, may hold values from -0.21875 to 0.21875
- step_bias: float32 [12], replicated, may hold values from -3 to -1
- decay_rate: float32 [12], replicated, may hold values from 0.0001 to 0.5, as said below
- conv_weight: float32 [4, 1024], replicated, may hold values from -3 to 3
- conv_bias: float32 [1024], replicated, may hold values from -3 to 3
- skip_gain: float32 [12], replicated, may hold values from 0.5 to 1.5
- norm_gain: float32 [768], replicated, may hold values from 0.5 to 1.5
- w_out: bfloat16 [768, 768], replicated, may hold values from -0.21875 to 0.21875
Outputs:
- mixed_out: bfloat16 [8192, 768], P(('dp', 'ctx')), parts along dimension 0
The draws below stay inside these ranges and needn't reach their ends.
There are 2 independent parts, one for each index of `dp`. The reference program is written for one: setup_inputs(seed, part) draws one part's arguments, and reference() takes and returns one part's arrays. A program takes and returns all parts, laid end to end along the dimension named above; an argument that names none is the same for every part. Nothing has to cross between parts.
Inputs may be any that keep to these rules, and one draw needn't show every extreme that they name: `base_ids`: base codes. `complement`: each code appears once. `decay_rate`: positive per-head rates.
All inputs are finite; a program needn't handle non-finite values.
Results may differ from the reference program's by a relative error of at most 0.0062.
Values may be sent and summed in bfloat16 or wider, within the bound.
No kernel may reach another device: no remote copies, remote signals or barrier semaphores. Data moves between devices by JAX's collectives and lax.ppermute only.
A program may use at most 256 MiB of HBM per device.

```python
import math
import jax
import jax.numpy as jnp
from jax import lax

D = 768
HEADS = 12
HEAD_DIM = 64
STATE = 128
CONV = 4
VOCAB = 5
INNER = 768
MIX = 1024
SEQ = 4096


def draw_decay_rate(key, part):
    low_end = 0.0001
    high_end = 0.5
    uniform_draw = jax.random.uniform(key, (HEADS,), jnp.float32)
    return jnp.exp(jnp.log(low_end) + uniform_draw * (jnp.log(high_end) - jnp.log(low_end))).astype(jnp.float32)


def set_ends(drawn, stream_key, smallest, high):
    extent = drawn.shape
    spot = [jax.random.randint(jax.random.fold_in(stream_key, axis), (), 0, extent[axis]) for axis in range(len(extent))]
    drawn = drawn.at[tuple(spot)].set(smallest)
    longest = extent.index(max(extent))
    spot[longest] = (spot[longest] + 1) % extent[longest]
    return drawn.at[tuple(spot)].set(high)


def bell_draw(rng, extent, width, limit, kind=jnp.bfloat16):
    values = width * jax.random.normal(rng, extent, jnp.float32)
    return jnp.clip(values, min=-limit, max=limit).astype(kind)


def setup_inputs(seed: int = 0, part: int = 0) -> dict:
    key_of = jax.random.split(jax.random.key(seed), 14)
    own_keys = jax.random.split(jax.random.fold_in(key_of[13], part), 14)
    base_ids = set_ends(jax.random.randint(own_keys[0], (SEQ,), 0, VOCAB), jax.random.fold_in(own_keys[0], 1), 0, VOCAB - 1).astype(jnp.int32)
    complement = jax.random.permutation(key_of[1], VOCAB).astype(jnp.int32)
    embedding = bell_draw(key_of[2], (VOCAB, D), 1.0, 6.0)
    w_gate = bell_draw(key_of[3], (D, INNER), D ** -0.5, 0.21875)
    w_mix = bell_draw(key_of[4], (D, MIX), D ** -0.5, 0.21875)
    w_step = bell_draw(key_of[5], (D, HEADS), D ** -0.5, 0.21875)
    step_bias = jnp.clip(jax.random.uniform(key_of[6], (HEADS,), jnp.float32, -3.0, -1.0), -3.0, -1.0)
    decay_rate = draw_decay_rate(jax.random.fold_in(key_of[13], 71), part)
    conv_weight = bell_draw(key_of[8], (CONV, MIX), 0.5, 3.0, jnp.float32)
    conv_bias = bell_draw(key_of[9], (MIX,), 0.5, 3.0, jnp.float32)
    skip_gain = jnp.clip(jax.random.uniform(key_of[10], (HEADS,), jnp.float32, 0.5, 1.5), 0.5, 1.5)
    norm_gain = jnp.clip(1.0 + 0.1 * jax.random.normal(key_of[11], (INNER,), jnp.float32), 0.5, 1.5)
    w_out = bell_draw(key_of[12], (INNER, D), INNER ** -0.5, 0.21875)
    return dict(base_ids=base_ids, complement=complement, embedding=embedding, w_gate=w_gate, w_mix=w_mix, w_step=w_step, step_bias=step_bias, decay_rate=decay_rate, conv_weight=conv_weight, conv_bias=conv_bias, skip_gain=skip_gain, norm_gain=norm_gain, w_out=w_out)


exact_mode = lax.Precision.HIGHEST

def block_pass(carry_pair, inputs):
    carried_state, offset = carry_pair
    values, keys_b, reads_c, log_decay, step_sizes = inputs
    cumulative = jnp.cumsum(log_decay, axis=0)
    headwise = jnp.transpose(cumulative)
    gaps_log = headwise[:, :, None] - headwise[:, None, :]
    block_size = cumulative.shape[0]
    causal = (jnp.arange(block_size)[:, None] >= jnp.arange(block_size)[None, :])[None]
    decays = jnp.where(causal, jnp.exp(jnp.where(causal, gaps_log, 0.0)), 0.0)
    scores = jnp.dot(reads_c, keys_b.T, precision=exact_mode)
    weights = scores[None] * decays * jnp.transpose(step_sizes)[:, None, :]
    inner_out = jnp.einsum('hts,shp->thp', weights, values, precision=exact_mode)
    carried = jnp.exp(cumulative)[:, :, None] * jnp.einsum('tn,hpn->thp', reads_c, carried_state, precision=exact_mode)
    tail_weight = jnp.exp(cumulative[-1][None, :] - cumulative) * step_sizes
    weighted_values = tail_weight[:, :, None] * values
    carried_state = jnp.exp(cumulative[-1])[:, None, None] * carried_state + jnp.einsum('shp,sn->hpn', weighted_values, keys_b, precision=exact_mode)
    return ((carried_state, offset + cumulative[-1]), (inner_out + carried, offset[None, :] + cumulative))

def strand_pass(ident_rows, mix_table, gate_table, step_table, step_bias, decay_rate, conv_weight, conv_bias, skip_gain, norm_gain):
    mixed = jnp.take(mix_table, ident_rows, axis=0).astype(jnp.float32)
    tap_count = conv_weight.shape[0]
    padded = jnp.concatenate([jnp.zeros((tap_count - 1, MIX), jnp.float32), mixed], axis=0)
    summed = conv_bias[None, :] + sum((conv_weight[tap_index][None, :] * padded[tap_index:tap_index + SEQ] for tap_index in range(tap_count)))
    conv_out = jax.nn.silu(summed)
    values = conv_out[:, :INNER].reshape(SEQ, HEADS, HEAD_DIM)
    keys_b = conv_out[:, INNER:INNER + STATE]
    reads_c = conv_out[:, INNER + STATE:]
    step_sizes = jax.nn.softplus(jnp.take(step_table, ident_rows, axis=0) + step_bias[None, :])
    log_decay = -step_sizes * decay_rate[None, :]
    block_rows = math.gcd(SEQ, 256)
    block_count = SEQ // block_rows
    shaped = (values.reshape(block_count, block_rows, HEADS, HEAD_DIM), keys_b.reshape(block_count, block_rows, STATE), reads_c.reshape(block_count, block_rows, STATE), log_decay.reshape(block_count, block_rows, HEADS), step_sizes.reshape(block_count, block_rows, HEADS))
    initial = (jnp.zeros((HEADS, HEAD_DIM, STATE), jnp.float32), jnp.zeros((HEADS,), jnp.float32))
    finals, outputs = lax.scan(block_pass, initial, shaped)
    partial_value = outputs[0].reshape(SEQ, HEADS, HEAD_DIM)
    ssm_out = partial_value + skip_gain[None, :, None] * values
    gated = ssm_out.reshape(SEQ, INNER) * jax.nn.silu(jnp.take(gate_table, ident_rows, axis=0).astype(jnp.float32))
    inverse_rms = lax.rsqrt(lax.optimization_barrier(jnp.mean(gated * gated, axis=1, keepdims=True)) + 1e-05)
    return gated * inverse_rms * norm_gain[None, :]

def reference(base_ids, complement, embedding, w_gate, w_mix, w_step, step_bias, decay_rate, conv_weight, conv_bias, skip_gain, norm_gain, w_out):
    gate_table = jnp.dot(embedding, w_gate, preferred_element_type=jnp.float32).astype(jnp.bfloat16)
    mix_table = jnp.dot(embedding, w_mix, preferred_element_type=jnp.float32).astype(jnp.bfloat16)
    step_table = jnp.dot(embedding, w_step, preferred_element_type=jnp.float32)

    def both_ways(ident_rows):
        forward = strand_pass(ident_rows, mix_table, gate_table, step_table, step_bias, decay_rate, conv_weight, conv_bias, skip_gain, norm_gain)
        backward = strand_pass(ident_rows[::-1], mix_table, gate_table, step_table, step_bias, decay_rate, conv_weight, conv_bias, skip_gain, norm_gain)[::-1]
        return (forward + backward).astype(jnp.bfloat16)
    second = jnp.take(complement, base_ids)[::-1].astype(jnp.int32)
    first_sum = both_ways(base_ids)
    second_sum = both_ways(second)[::-1]
    result = jnp.dot(first_sum, w_out, preferred_element_type=jnp.float32) + jnp.dot(second_sum, w_out, preferred_element_type=jnp.float32)
    return result.astype(jnp.bfloat16)
```

```python
import functools

import jax
import jax.numpy as jnp
from jax import lax
from jax.experimental import pallas as pl
from jax.experimental.pallas import tpu as pltpu
from jax.sharding import PartitionSpec as P

F32, BF16, I32 = jnp.float32, jnp.bfloat16, jnp.int32
LETTER_ROWS = 8
CHUNK = 128
VMEM = pltpu.VMEM


def dot(a, b, contract=((1,), (0,))):
    return lax.dot_general(a, b, (contract, ((), ())), preferred_element_type=F32)


TN = ((0,), (0,))
NT = ((1,), (1,))


def silu(x):
    half = 0.5 * x
    return half + half * jnp.tanh(half)


def split(x):
    high = x.astype(BF16).astype(F32)
    return high, x - high


def iota(shape, dim):
    return lax.broadcasted_iota(I32, shape, dim)


def onehot_rows(row):
    return jnp.where(jnp.broadcast_to(row, (LETTER_ROWS, row.shape[1])) == iota((LETTER_ROWS, row.shape[1]), 0), 1.0, 0.0)


def code_onehot(shape, code_dim):
    code, slot = iota(shape, code_dim), iota(shape, 1 - code_dim) & 31
    before, last = code & 127, code >> 7
    first = (before * 41) >> 10
    pair = (before * 205) >> 10
    second, third = pair - 5 * first, before - 5 * pair
    tap = slot >> 3
    digit = jnp.where(tap == 0, first, jnp.where(tap == 1, second, jnp.where(tap == 2, third, last)))
    return jnp.where(digit == (slot & 7), 1.0, 0.0).astype(BF16)


def head_spread(rows, columns, head_dim):
    low = iota((rows, columns), 0) * head_dim
    lane = iota((rows, columns), 1)
    return jnp.where((lane >= low) & (lane < low + head_dim), 1.0, 0.0)


def tables_kernel(
    comp, emb, w_gate, w_mix, w_step, step_bias, rate, conv_w, conv_b, skip,
    taps, taps_t, look, ldt, stept, stepk, skipx, xt, bt,
    e16, *, heads, head_dim, state,
):
    letters, inner = emb.shape[0], heads * head_dim
    e16[...] = jnp.zeros_like(e16)
    e16[0:letters, :] = emb[...].astype(F32)
    for v in range(letters):
        e16[LETTER_ROWS + v : LETTER_ROWS + v + 1, :] = e16[pl.ds(comp[v], 1), :]
    rows = e16[...].astype(BF16)
    mix = dot(rows, w_mix[...]).astype(BF16).astype(F32)
    gate = silu(dot(rows, w_gate[...]).astype(BF16).astype(F32))
    raw = dot(rows, w_step[...]) + step_bias[...]
    step = jnp.maximum(raw, 0.0) + jnp.log1p(jnp.exp(-jnp.abs(raw)))
    decay_t = jnp.transpose(-step * rate[...])
    step_t = jnp.transpose(step)
    for strand in range(2):
        at = slice(strand * LETTER_ROWS, (strand + 1) * LETTER_ROWS)
        ldt[strand * heads : (strand + 1) * heads, :] = decay_t[:, at]
        stept[strand * heads : (strand + 1) * heads, :] = step_t[:, at]
        for v in range(letters):
            stepk[strand * heads : (strand + 1) * heads, v * 128 : (v + 1) * 128] = jnp.broadcast_to(
                step_t[:, strand * LETTER_ROWS + v : strand * LETTER_ROWS + v + 1], (heads, 128)
            )
    spread = head_spread(heads, inner, head_dim).astype(BF16)
    for part, high_low in enumerate(split(step)):
        wide = dot(high_low.astype(BF16), spread)
        for strand in range(2):
            at = slice(strand * LETTER_ROWS, (strand + 1) * LETTER_ROWS)
            look[part * LETTER_ROWS : (part + 1) * LETTER_ROWS, (2 + strand) * inner : (3 + strand) * inner] = wide[at]
    for part, high_low in enumerate(split(gate)):
        for strand in range(2):
            at = slice(strand * LETTER_ROWS, (strand + 1) * LETTER_ROWS)
            look[part * LETTER_ROWS : (part + 1) * LETTER_ROWS, strand * inner : (strand + 1) * inner] = high_low[at]
    skip_high, skip_rest = split(skip[...])
    skip_mid, skip_low = split(skip_rest)
    skipx[...] = sum(dot(part.astype(BF16), spread) for part in (skip_high, skip_mid, skip_low))
    width = conv_w.shape[1]
    codes = xt.shape[2]
    by_column = code_onehot((64, codes), 1)
    by_row = code_onehot((codes, 64), 0)
    for strand in range(2):
        letter_rows = mix[strand * LETTER_ROWS : (strand + 1) * LETTER_ROWS]
        weighted = [conv_w[k : k + 1, :] * letter_rows for k in range(4)]
        weighted[3] = weighted[3] + conv_b[...]
        high, low = split(jnp.concatenate(weighted, axis=0))
        both = jnp.concatenate([high, low], axis=0)
        taps[:, strand * width : (strand + 1) * width] = both.astype(BF16)
        turned = jnp.transpose(both[:, :inner]).astype(BF16)
        taps_t[strand] = turned
        for low_row in range(0, inner, CHUNK):
            xt[strand, low_row : low_row + CHUNK, :] = silu(dot(turned[low_row : low_row + CHUNK], by_column)).astype(BF16)
        bt[strand] = silu(dot(by_row, both[:, inner : inner + state].astype(BF16))).astype(BF16)


def local_kernel(
    near, taps, look, ldt, skipx,
    yg, eg, reads,
    *, heads, head_dim, state,
):
    length, inner = near.shape[1], heads * head_dim
    width = inner + 2 * state
    blocks = length // CHUNK
    ahead = jnp.concatenate([onehot_rows(near[k : k + 1, :]) for k in range(4)] * 2, axis=0).astype(BF16)
    behind = jnp.concatenate([onehot_rows(near[6 - k : 7 - k, :]) for k in range(4)] * 2, axis=0).astype(BF16)
    own = onehot_rows(near[3:4, :])
    own2 = jnp.concatenate([own, own], axis=0).astype(BF16)
    upto = jnp.where(iota((length, length), 0) <= iota((length, length), 1), 1.0, 0.0).astype(BF16)
    count = dot(own.astype(BF16), upto)
    before = count - own
    ld = ldt[...]
    full = sum(ld[:, v : v + 1] * count[v : v + 1, :] for v in range(5))
    less = sum(ld[:, v : v + 1] * before[v : v + 1, :] for v in range(5))
    full_t, less_t = jnp.transpose(full), jnp.transpose(less)
    spread = head_spread(2 * heads, 2 * inner, head_dim)
    spread = jnp.concatenate([spread, spread], axis=0).astype(BF16)
    enter = (jnp.exp(full), jnp.exp(full[:, length - 1 : length] - less))
    enter = [jnp.concatenate(split(part), axis=0).astype(BF16) for part in enter]
    row, lane = iota((CHUNK, CHUNK), 0), iota((CHUNK, CHUNK), 1)
    lower, upper = row >= lane, row <= lane
    first_half = iota((CHUNK, CHUNK), 1) < head_dim
    span = lambda i: slice(i * CHUNK, (i + 1) * CHUNK)
    for strand in range(2):
        gate = dot(own2, look[:, strand * inner : (strand + 1) * inner], TN)
        stepx = dot(own2, look[:, (2 + strand) * inner : (3 + strand) * inner], TN)
        values, stepped, scores = [], [], []
        for way, hot in enumerate((ahead, behind)):
            conv = silu(dot(hot, taps[:, strand * width : (strand + 1) * width], TN))
            x = conv[:, :inner]
            keys, read = conv[:, inner : inner + state].astype(BF16), conv[:, inner + state :].astype(BF16)
            reads[2 * strand + way] = read
            values.append(x)
            stepped.append((x * stepx).astype(BF16))
            scores.append(dot(read, keys, NT))
            eg[2 * strand + way] = (
                dot(enter[way], spread[:, strand * inner : (strand + 1) * inner], TN) * gate
            ).astype(BF16)
        cut = {}
        for i in range(blocks):
            for j in range(blocks):
                if i >= j:
                    s = scores[0][span(i), span(j)]
                    cut[0, i, j] = jnp.where(lower, s, 0.0) if i == j else s
                if i <= j:
                    s = scores[1][span(i), span(j)]
                    cut[1, i, j] = jnp.where(upper, s, 0.0) if i == j else s
        for pair in range(heads // 2):
            columns = slice(pair * 2 * head_dim, (pair + 1) * 2 * head_dim)
            found = []
            for head in (2 * pair, 2 * pair + 1):
                k = strand * heads + head
                decay = {}
                for i in range(blocks):
                    for j in range(blocks):
                        if i >= j:
                            down = full_t[span(i), k : k + 1] - full[k : k + 1, span(j)]
                        if i <= j:
                            up = less[k : k + 1, span(j)] - less_t[span(i), k : k + 1]
                        gap = down if i > j else up if i < j else jnp.where(lower, down, up)
                        decay[i, j] = jnp.exp(gap)
                for way in range(2):
                    out = []
                    for i in range(blocks):
                        js = range(i + 1) if way == 0 else range(i, blocks)
                        weights = jnp.concatenate([(cut[way, i, j] * decay[i, j]).astype(BF16) for j in js], axis=1)
                        out.append(dot(weights, stepped[way][js[0] * CHUNK : (js[-1] + 1) * CHUNK, columns]))
                    found.append(out)
            for way in range(2):
                for i in range(blocks):
                    y = jnp.where(first_half, found[way][i], found[2 + way][i])
                    y = y + skipx[:, columns] * values[way][span(i), columns]
                    yg[2 * strand + way, span(i), columns] = y * gate[span(i), columns]


def finish_kernel(
    ids, ldt, stept, stepk, taps, taps_t, xt, bt, reads, yg, eg, norm_gain, w_out,
    out,
    *, heads, head_dim, state,
):
    members, length = ids.shape
    inner = heads * head_dim
    width = inner + 2 * state
    position = lax.axis_index("ctx")
    letters = 5
    every = ids[...]
    lane = iota((members, length), 1)
    block = iota((members, length), 0)
    prev, after = [], []
    up, down = pltpu.roll(every, 1, 0), pltpu.roll(every, members - 1, 0)
    for k in (1, 2, 3):
        inside, outside = pltpu.roll(every, k, 1), pltpu.roll(up, k, 1)
        found = jnp.where(lane >= k, inside, outside)
        prev.append(jnp.where((block == 0) & (lane < k), -1, found))
        inside, outside = pltpu.roll(every, length - k, 1), pltpu.roll(down, length - k, 1)
        found = jnp.where(lane < length - k, inside, outside)
        after.append(jnp.where((block == members - 1) & (lane >= length - k), -1, found))
    code_ahead = jnp.where((block == 0) & (lane < 3), -1, prev[2] * 25 + prev[1] * 5 + prev[0])
    code_behind = jnp.where((block == members - 1) & (lane >= length - 3), -1, after[2] * 25 + after[1] * 5 + after[0])
    code = jnp.where(block < position, code_ahead, code_behind)

    marks = [onehot_rows(every[b : b + 1, :]) for b in range(members)]
    mark = jnp.concatenate(marks, axis=0)
    rows = members * LETTER_ROWS
    its_block = iota((rows, 1), 0) >> 3
    i, j = iota((rows, rows), 0), iota((rows, rows), 1)
    bi, bj = i >> 3, j >> 3
    between = ((bi < bj) & (bj < position)) | ((position < bj) & (bj < bi))
    between = jnp.where(((i & 7) == (j & 7)) & between, 1.0, 0.0).astype(BF16)
    amid = dot(between, mark.astype(BF16)).astype(BF16)
    s, t = iota((length, length), 0), iota((length, length), 1)
    later = jnp.where(s > t, 1.0, 0.0).astype(BF16)
    earlier = jnp.where(s < t, 1.0, 0.0).astype(BF16)
    ones = jnp.ones((length, length), BF16)
    counts = (
        dot(jnp.where(its_block < position, mark, 0.0).astype(BF16), later)
        + dot(jnp.where(its_block > position, mark, 0.0).astype(BF16), earlier)
        + dot(amid, ones)
    )
    ld = ldt[...]
    weighed, hot, far = [], [], {}
    for b in range(members):
        count = counts[b * LETTER_ROWS : (b + 1) * LETTER_ROWS]
        far_b = jnp.exp(sum(ld[:, v : v + 1] * count[v : v + 1, :] for v in range(letters)))
        if b in (0, members - 1):
            far[b] = far_b
        by_last = [far_b * marks[b][v : v + 1, :] for v in range(letters)]
        in_front = jnp.where(b < position, 1.0, 0.0)
        in_back = jnp.where(b > position, 1.0, 0.0)
        by_last = [part * in_front for part in by_last] + [part * in_back for part in by_last]
        weighed.append(jnp.concatenate(by_last, axis=0).astype(BF16))
        hot.append(jnp.where(iota((128, length), 0) == code[b : b + 1, :], 1.0, 0.0).astype(BF16))
    sums = dot(jnp.concatenate(weighed, axis=1), jnp.concatenate(hot, axis=1), NT)

    edge_lane = iota((1, 128), 1)
    tail = slice(length - 128, length)
    digits = [jnp.where(edge_lane < 64, prev[2 - k][0:1, :128], after[2 - k][members - 1 :, tail]) for k in range(3)]
    digits.append(jnp.where(edge_lane < 64, every[0:1, :128], every[members - 1 :, tail]))
    edge_hot = jnp.concatenate([onehot_rows(d) for d in digits] * 2, axis=0).astype(BF16)
    st = stept[...]
    first_step = sum(st[:, v : v + 1] * marks[0][v : v + 1, :128] for v in range(letters))
    last_step = sum(st[:, v : v + 1] * marks[members - 1][v : v + 1, tail] for v in range(letters))
    edge_ahead = jnp.where((edge_lane < 3) & (position > 0), far[0][:, :128] * first_step, 0.0)
    edge_behind = jnp.where(
        (edge_lane >= 125) & (position < members - 1), far[members - 1][:, tail] * last_step, 0.0
    )
    span = 2 * heads
    total = jnp.zeros((length, inner), F32)
    weights = []
    for way, edge in enumerate((edge_ahead, edge_behind)):
        base = way * letters * span
        wide = jnp.concatenate([sums[base + v * span : base + (v + 1) * span] for v in range(letters)], axis=1)
        weights.append(jnp.concatenate([wide * stepk[...], edge], axis=1).astype(BF16))
    for strand in range(2):
        edge_x = silu(dot(taps_t[strand], edge_hot)).astype(BF16)
        edge_b = silu(dot(edge_hot, taps[:, strand * width + inner : strand * width + inner + state], TN)).astype(BF16)
        keys = jnp.concatenate([bt[strand], edge_b], axis=0)
        for way in range(2):
            scaled = []
            for head in range(heads):
                at = slice(head * head_dim, (head + 1) * head_dim)
                x_head = jnp.concatenate([xt[strand, at, :], edge_x[at]], axis=1)
                scaled.append(x_head * weights[way][strand * heads + head : strand * heads + head + 1, :])
            entering = dot(jnp.concatenate(scaled, axis=0), keys).astype(BF16)
            which = 2 * strand + way
            carried = dot(reads[which], entering, NT)
            g = yg[which] + carried * eg[which].astype(F32)
            power = jnp.sum(g * g, axis=1, keepdims=True) * (1.0 / inner)
            total = total + g * lax.rsqrt(power + 1e-05)
    out[...] = dot((total * norm_gain[...]).astype(BF16), w_out[...]).astype(BF16)


def on_device(
    base_ids, complement, embedding, w_gate, w_mix, w_step, step_bias, decay_rate,
    conv_weight, conv_bias, skip_gain, norm_gain, w_out,
):
    length = base_ids.shape[0]
    heads = decay_rate.shape[0]
    inner = w_gate.shape[1]
    head_dim = inner // heads
    width = w_mix.shape[1]
    state = (width - inner) // 2
    members = lax.axis_size("ctx")
    position = lax.axis_index("ctx")
    sizes = dict(heads=heads, head_dim=head_dim, state=state)
    letters = embedding.shape[0]
    codes = letters * 128
    vmem = pl.BlockSpec(memory_space=VMEM)
    params = pltpu.CompilerParams(vmem_limit_bytes=24 * 1024 * 1024)

    odd = position % 2 == 1
    own = base_ids.reshape(1, length)
    across = [(i, (i + 1) % members if i % 2 else (i - 1) % members) for i in range(members)]
    other = lax.ppermute(own, "ctx", across)
    two = jnp.where(odd, jnp.concatenate([own, other]), jnp.concatenate([other, own]))
    got = lax.ppermute(two, "ctx", [(i, i ^ 1) for i in range(members)])
    window = jnp.where(odd, jnp.concatenate([got, two]), jnp.concatenate([two, got]))
    left = jnp.where(odd, window[1:2], window[0:1])[:, length - 3 :]
    right = jnp.where(odd, window[3:4], window[2:3])[:, :3]
    left = jnp.where(position == 0, -1, left)
    right = jnp.where(position == members - 1, -1, right)
    extended = jnp.concatenate([left, own, right, jnp.zeros((1, 1), I32)], axis=1)
    near = jnp.concatenate([extended[:, k : k + length] for k in range(7)] + [own], axis=0)

    bit = 4
    ids = window
    while bit < members:
        got = lax.ppermute(ids, "ctx", [(i, i ^ bit ^ 1) for i in range(members)])
        ids = jnp.where(position & bit == 0, jnp.concatenate([ids, got]), jnp.concatenate([got, ids]))
        bit *= 2
    ids = jnp.where(position & 2 == 0, jnp.roll(ids, -1, axis=0), jnp.roll(ids, 1, axis=0))

    smem = pl.BlockSpec(memory_space=pltpu.SMEM)
    row = lambda a: a.reshape(1, -1)
    shape = jax.ShapeDtypeStruct
    taps, taps_t, look, ldt, stept, stepk, skipx, xt, bt = pl.pallas_call(
        functools.partial(tables_kernel, **sizes),
        out_shape=[
            shape((64, 2 * width), BF16),
            shape((2, inner, 64), BF16),
            shape((2 * LETTER_ROWS, 4 * inner), F32),
            shape((2 * heads, LETTER_ROWS), F32),
            shape((2 * heads, LETTER_ROWS), F32),
            shape((2 * heads, codes), F32),
            shape((1, inner), F32),
            shape((2, inner, codes), BF16),
            shape((2, codes, state), BF16),
        ],
        in_specs=[smem] + [vmem] * 9,
        out_specs=[vmem] * 9,
        scratch_shapes=[VMEM((2 * LETTER_ROWS, embedding.shape[1]), F32)],
        compiler_params=params,
        name="tables",
    )(
        complement, embedding, w_gate, w_mix, w_step, row(step_bias), row(decay_rate), conv_weight,
        row(conv_bias), row(skip_gain),
    )
    look = look.astype(BF16)

    yg, eg, reads = pl.pallas_call(
        functools.partial(local_kernel, **sizes),
        out_shape=[
            shape((4, length, inner), F32),
            shape((4, length, inner), BF16),
            shape((4, length, state), BF16),
        ],
        in_specs=[vmem] * 5,
        out_specs=[vmem] * 3,
        compiler_params=params,
        name="local",
    )(near, taps, look, ldt, skipx)

    return pl.pallas_call(
        functools.partial(finish_kernel, **sizes),
        out_shape=shape((length, w_out.shape[1]), BF16),
        in_specs=[vmem] * 13,
        out_specs=vmem,
        compiler_params=params,
        name="finish",
    )(ids, ldt, stept, stepk, taps, taps_t, xt, bt, reads, yg, eg, row(norm_gain), w_out)


def solution(mesh):
    return jax.shard_map(
        on_device,
        mesh=mesh,
        in_specs=(P(("dp", "ctx")), P(), P(), P(), P(), P(), P(), P(), P(), P(), P(), P(), P()),
        out_specs=P(("dp", "ctx"), None),
        check_vma=False,
    )
```

```python
import functools

import jax
import jax.numpy as jnp
from jax import lax
from jax.experimental import pallas as pl
from jax.experimental.pallas import tpu as pltpu
from jax.sharding import PartitionSpec as P

F32, BF16, I32 = jnp.float32, jnp.bfloat16, jnp.int32
LETTER_ROWS = 8
CHUNK = 128
VMEM = pltpu.VMEM
VMEM_LIMIT = 24 * 1024 * 1024
DECAY_AT, STEP_AT, GAIN_AT = 768, 896, 32


def dot(a, b, contract=((1,), (0,))):
    return lax.dot_general(a, b, (contract, ((), ())), preferred_element_type=F32)


TN = ((0,), (0,))
NT = ((1,), (1,))


def silu(x):
    half = 0.5 * x
    return half + half * jnp.tanh(half)


def split(x):
    high = x.astype(BF16).astype(F32)
    return high, x - high


def iota(shape, dim):
    return lax.broadcasted_iota(I32, shape, dim)


def onehot_rows(row):
    return jnp.where(jnp.broadcast_to(row, (LETTER_ROWS, row.shape[1])) == iota((LETTER_ROWS, row.shape[1]), 0), 1.0, 0.0)


def code_onehot(shape, code_dim):
    code, slot = iota(shape, code_dim), iota(shape, 1 - code_dim) & 31
    before, last = code & 127, code >> 7
    first = (before * 41) >> 10
    pair = (before * 205) >> 10
    second, third = pair - 5 * first, before - 5 * pair
    tap = slot >> 3
    digit = jnp.where(tap == 0, first, jnp.where(tap == 1, second, jnp.where(tap == 2, third, last)))
    return jnp.where(digit == (slot & 7), 1.0, 0.0).astype(BF16)


def head_spread(rows, columns, head_dim):
    low = iota((rows, columns), 0) * head_dim
    lane = iota((rows, columns), 1)
    return jnp.where((lane >= low) & (lane < low + head_dim), 1.0, 0.0)


def tables_kernel(
    base_ids_h, comp_h, emb_h, w_gate_h, w_mix_h, w_step_h, step_bias_h, rate_h, conv_w_h, conv_b_h, skip_h,
    norm_gain_h,
    own, wide, xt, small,
    e16, ids_v, comp, emb, w_gate, w_mix, w_step, step_bias, rate, conv_w, conv_b, skip, gain_v, sems,
    *, heads, head_dim, state,
):
    pairs = [
        (emb_h, emb), (comp_h, comp), (w_mix_h, w_mix), (w_step_h, w_step), (step_bias_h, step_bias), (rate_h, rate),
        (skip_h, skip), (conv_w_h, conv_w), (conv_b_h, conv_b), (w_gate_h, w_gate), (base_ids_h, ids_v),
        (norm_gain_h, gain_v),
    ]
    copies = [pltpu.make_async_copy(a, b, sems.at[n]) for n, (a, b) in enumerate(pairs)]
    for copy in copies:
        copy.start()
    letters, inner = emb.shape[0], heads * head_dim
    e16[...] = jnp.zeros_like(e16)
    copies[0].wait()
    copies[1].wait()
    e16[0:letters, :] = emb[...].astype(F32)
    for v in range(letters):
        e16[LETTER_ROWS + v : LETTER_ROWS + v + 1, :] = e16[pl.ds(comp[v], 1), :]
    rows = e16[...].astype(BF16)
    for copy in copies[2:9]:
        copy.wait()
    mix = dot(rows, w_mix[...]).astype(BF16).astype(F32)
    raw = dot(rows, w_step[...], NT) + step_bias[...].reshape(1, heads)
    step = jnp.maximum(raw, 0.0) + jnp.log1p(jnp.exp(-jnp.abs(raw)))
    decay_t = jnp.transpose(-step * rate[...].reshape(1, heads))
    step_t = jnp.transpose(step)
    for strand in range(2):
        at = slice(strand * LETTER_ROWS, (strand + 1) * LETTER_ROWS)
        small[strand * heads : (strand + 1) * heads, DECAY_AT : DECAY_AT + LETTER_ROWS] = decay_t[:, at]
        small[strand * heads : (strand + 1) * heads, STEP_AT : STEP_AT + LETTER_ROWS] = step_t[:, at]
        for v in range(letters):
            small[strand * heads : (strand + 1) * heads, v * 128 : (v + 1) * 128] = jnp.broadcast_to(
                step_t[:, strand * LETTER_ROWS + v : strand * LETTER_ROWS + v + 1], (heads, 128)
            )
    spread = head_spread(heads, inner, head_dim).astype(BF16)
    steps = [dot(part.astype(BF16), spread) for part in split(step)]
    skip_high, skip_rest = split(skip[...].reshape(1, heads))
    skip_mid, skip_low = split(skip_rest)
    small[2 * heads : 2 * heads + 1, :inner] = sum(dot(part.astype(BF16), spread) for part in (skip_high, skip_mid, skip_low))
    width, codes = conv_w.shape[1], xt.shape[2]
    by_column = code_onehot((64, codes), 1)
    for strand in range(2):
        letter_rows = mix[strand * LETTER_ROWS : (strand + 1) * LETTER_ROWS]
        weighted = [conv_w[k : k + 1, :] * letter_rows for k in range(4)]
        weighted[3] = weighted[3] + conv_b[...].reshape(1, -1)
        high, low = split(jnp.concatenate(weighted, axis=0))
        both = jnp.concatenate([high, low], axis=0)
        wide[strand, :, :width] = both.astype(BF16)
        across = jnp.transpose(both[:, : inner + state]).astype(BF16)
        for low_row in range(0, inner + state, CHUNK):
            xt[strand, low_row : low_row + CHUNK, :] = silu(dot(across[low_row : low_row + CHUNK], by_column)).astype(BF16)
    copies[9].wait()
    gate = silu(dot(rows, w_gate[...]).astype(BF16).astype(F32))
    gates = split(gate)
    for strand in range(2):
        at = slice(strand * LETTER_ROWS, (strand + 1) * LETTER_ROWS)
        rest = jnp.zeros((3 * LETTER_ROWS, 2 * inner), F32)
        parts = [jnp.concatenate([gates[n][at], steps[n][at]], axis=1) for n in range(2)]
        wide[strand, :, width:] = jnp.concatenate([rest, parts[0], rest, parts[1]], axis=0).astype(BF16)
    for copy in copies[10:]:
        copy.wait()
    own[...] = ids_v[...].reshape(own.shape)
    small[GAIN_AT : GAIN_AT + 1, :inner] = gain_v[...].reshape(1, inner)


def local_kernel(
    window, wide, small, *rest,
    strand, heads, head_dim, state,
):
    yg, eg, reads = rest[-3:]
    length, inner = window.shape[1], heads * head_dim
    blocks = length // CHUNK
    members, position = lax.axis_size("ctx"), lax.axis_index("ctx")
    odd = position % 2 == 1
    here = jnp.where(odd, window[2:3, :], window[1:2, :])
    back = jnp.where(position == 0, -1, jnp.where(odd, window[1:2, :], window[0:1, :]))
    fore = jnp.where(position == members - 1, -1, jnp.where(odd, window[3:4, :], window[2:3, :]))
    place = iota((1, length), 1)
    rows_behind, rows_ahead = [here], [here]
    for k in (1, 2, 3):
        rows_behind.append(jnp.where(place >= k, pltpu.roll(here, k, 1), pltpu.roll(back, k, 1)))
        rows_ahead.append(
            jnp.where(place < length - k, pltpu.roll(here, length - k, 1), pltpu.roll(fore, length - k, 1))
        )
    ahead = jnp.concatenate([onehot_rows(r) for r in rows_behind[::-1]] * 2, axis=0).astype(BF16)
    behind = jnp.concatenate([onehot_rows(r) for r in rows_ahead[::-1]] * 2, axis=0).astype(BF16)
    own = onehot_rows(here)
    upto = jnp.where(iota((length, length), 0) <= iota((length, length), 1), 1.0, 0.0).astype(BF16)
    count = dot(own.astype(BF16), upto)
    before = count - own
    ld = small[strand * heads : (strand + 1) * heads, DECAY_AT : DECAY_AT + LETTER_ROWS]
    skipx = small[2 * heads : 2 * heads + 1, :inner]
    width = inner + 2 * state
    full = sum(ld[:, v : v + 1] * count[v : v + 1, :] for v in range(5))
    less = sum(ld[:, v : v + 1] * before[v : v + 1, :] for v in range(5))
    full_t, less_t = jnp.transpose(full), jnp.transpose(less)
    spread = head_spread(heads, inner, head_dim)
    spread = spread.astype(BF16)
    enter = (jnp.exp(full), jnp.exp(full[:, length - 1 : length] - less))
    enter = [[half.astype(BF16) for half in split(part)] for part in enter]
    row, lane = iota((CHUNK, CHUNK), 0), iota((CHUNK, CHUNK), 1)
    lower, upper = row >= lane, row <= lane
    first_half = iota((CHUNK, CHUNK), 1) < head_dim
    span = lambda i: slice(i * CHUNK, (i + 1) * CHUNK)
    gate = dot(ahead, wide[strand, :, width : width + inner], TN)
    stepx = dot(ahead, wide[strand, :, width + inner :], TN)
    values, stepped, scores = [], [], []
    for way, hot in enumerate((ahead, behind)):
        conv = silu(dot(hot, wide[strand, :, :width], TN))
        x = conv[:, :inner]
        keys, read = conv[:, inner : inner + state].astype(BF16), conv[:, inner + state :].astype(BF16)
        reads[way] = read
        values.append(x)
        stepped.append((x * stepx).astype(BF16))
        scores.append(dot(read, keys, NT))
        eg[way] = (
            sum(dot(half, spread, TN) for half in enter[way]) * gate
        ).astype(BF16)
    cut = {}
    for i in range(blocks):
        for j in range(blocks):
            if i >= j:
                s = scores[0][span(i), span(j)]
                cut[0, i, j] = jnp.where(lower, s, 0.0) if i == j else s
            if i <= j:
                s = scores[1][span(i), span(j)]
                cut[1, i, j] = jnp.where(upper, s, 0.0) if i == j else s
    for pair in range(heads // 2):
        columns = slice(pair * 2 * head_dim, (pair + 1) * 2 * head_dim)
        found = []
        for head in (2 * pair, 2 * pair + 1):
            k = head
            decay = {}
            for i in range(blocks):
                for j in range(blocks):
                    if i >= j:
                        down = full_t[span(i), k : k + 1] - full[k : k + 1, span(j)]
                    if i <= j:
                        up = less[k : k + 1, span(j)] - less_t[span(i), k : k + 1]
                    gap = down if i > j else up if i < j else jnp.where(lower, down, up)
                    decay[i, j] = jnp.exp(gap)
            for way in range(2):
                out = []
                for i in range(blocks):
                    js = range(i + 1) if way == 0 else range(i, blocks)
                    weights = jnp.concatenate([(cut[way, i, j] * decay[i, j]).astype(BF16) for j in js], axis=1)
                    out.append(dot(weights, stepped[way][js[0] * CHUNK : (js[-1] + 1) * CHUNK, columns]))
                found.append(out)
        for way in range(2):
            for i in range(blocks):
                y = jnp.where(first_half, found[way][i], found[2 + way][i])
                y = y + skipx[:, columns] * values[way][span(i), columns]
                yg[way, span(i), columns] = y * gate[span(i), columns]


def finish_kernel(
    ids, wide, xt, small, reads0, yg0, eg0, reads1, yg1, eg1, w_out_h,
    out,
    w_out, sem,
    *, heads, head_dim, state,
):
    members, length = ids.shape
    inner = heads * head_dim
    position = lax.axis_index("ctx")
    letters = 5
    load = pltpu.make_async_copy(w_out_h, w_out, sem)
    load.start()
    every = ids[...]
    lane = iota((members, length), 1)
    block = iota((members, length), 0)
    prev, after = [], []
    up, down = pltpu.roll(every, 1, 0), pltpu.roll(every, members - 1, 0)
    for k in (1, 2, 3):
        inside, outside = pltpu.roll(every, k, 1), pltpu.roll(up, k, 1)
        found = jnp.where(lane >= k, inside, outside)
        prev.append(jnp.where((block == 0) & (lane < k), -1, found))
        inside, outside = pltpu.roll(every, length - k, 1), pltpu.roll(down, length - k, 1)
        found = jnp.where(lane < length - k, inside, outside)
        after.append(jnp.where((block == members - 1) & (lane >= length - k), -1, found))
    code_ahead = jnp.where((block == 0) & (lane < 3), -1, prev[2] * 25 + prev[1] * 5 + prev[0])
    code_behind = jnp.where((block == members - 1) & (lane >= length - 3), -1, after[2] * 25 + after[1] * 5 + after[0])
    code = jnp.where(block < position, code_ahead, code_behind)

    marks = [onehot_rows(every[b : b + 1, :]) for b in range(members)]
    mark = jnp.concatenate(marks, axis=0)
    rows = members * LETTER_ROWS
    its_block = iota((rows, 1), 0) >> 3
    i, j = iota((rows, rows), 0), iota((rows, rows), 1)
    bi, bj = i >> 3, j >> 3
    between = ((bi < bj) & (bj < position)) | ((position < bj) & (bj < bi))
    between = jnp.where(((i & 7) == (j & 7)) & between, 1.0, 0.0).astype(BF16)
    amid = dot(between, mark.astype(BF16)).astype(BF16)
    s, t = iota((length, length), 0), iota((length, length), 1)
    later = jnp.where(s > t, 1.0, 0.0).astype(BF16)
    earlier = jnp.where(s < t, 1.0, 0.0).astype(BF16)
    ones = jnp.ones((length, length), BF16)
    counts = (
        dot(jnp.where(its_block < position, mark, 0.0).astype(BF16), later)
        + dot(jnp.where(its_block > position, mark, 0.0).astype(BF16), earlier)
        + dot(amid, ones)
    )
    ld = small[: 2 * heads, DECAY_AT : DECAY_AT + LETTER_ROWS]
    weighed, hot, far = [], [], {}
    for b in range(members):
        count = counts[b * LETTER_ROWS : (b + 1) * LETTER_ROWS]
        far_b = jnp.exp(sum(ld[:, v : v + 1] * count[v : v + 1, :] for v in range(letters)))
        if b in (0, members - 1):
            far[b] = far_b
        by_last = [far_b * marks[b][v : v + 1, :] for v in range(letters)]
        in_front = jnp.where(b < position, 1.0, 0.0)
        in_back = jnp.where(b > position, 1.0, 0.0)
        by_last = [part * in_front for part in by_last] + [part * in_back for part in by_last]
        weighed.append(jnp.concatenate(by_last, axis=0).astype(BF16))
        hot.append(jnp.where(iota((128, length), 0) == code[b : b + 1, :], 1.0, 0.0).astype(BF16))
    sums = dot(jnp.concatenate(weighed, axis=1), jnp.concatenate(hot, axis=1), NT)

    edge_lane = iota((1, 128), 1)
    tail = slice(length - 128, length)
    digits = [jnp.where(edge_lane < 64, prev[2 - k][0:1, :128], after[2 - k][members - 1 :, tail]) for k in range(3)]
    digits.append(jnp.where(edge_lane < 64, every[0:1, :128], every[members - 1 :, tail]))
    edge_hot = jnp.concatenate([onehot_rows(d) for d in digits] * 2, axis=0).astype(BF16)
    st = small[: 2 * heads, STEP_AT : STEP_AT + LETTER_ROWS]
    stepk = small[: 2 * heads, : letters * 128]
    first_step = sum(st[:, v : v + 1] * marks[0][v : v + 1, :128] for v in range(letters))
    last_step = sum(st[:, v : v + 1] * marks[members - 1][v : v + 1, tail] for v in range(letters))
    edge_ahead = jnp.where((edge_lane < 3) & (position > 0), far[0][:, :128] * first_step, 0.0)
    edge_behind = jnp.where(
        (edge_lane >= 125) & (position < members - 1), far[members - 1][:, tail] * last_step, 0.0
    )
    span = 2 * heads
    total = jnp.zeros((length, inner), F32)
    weights = []
    for way, edge in enumerate((edge_ahead, edge_behind)):
        base = way * letters * span
        by_code = jnp.concatenate([sums[base + v * span : base + (v + 1) * span] for v in range(letters)], axis=1)
        weights.append(jnp.concatenate([by_code * stepk, edge], axis=1).astype(BF16))
    for strand in range(2):
        edge = silu(dot(wide[strand, :, : inner + state], edge_hot, TN)).astype(BF16)
        keys = jnp.concatenate([xt[strand, inner:, :], edge[inner:]], axis=1)
        for way in range(2):
            scaled = []
            for head in range(heads):
                at = slice(head * head_dim, (head + 1) * head_dim)
                x_head = jnp.concatenate([xt[strand, at, :], edge[at]], axis=1)
                scaled.append(x_head * weights[way][strand * heads + head : strand * heads + head + 1, :])
            entering = dot(jnp.concatenate(scaled, axis=0), keys, NT).astype(BF16)
            reads, yg, eg = ((reads0, yg0, eg0), (reads1, yg1, eg1))[strand]
            carried = dot(reads[way], entering, NT)
            g = yg[way] + carried * eg[way].astype(F32)
            power = jnp.sum(g * g, axis=1, keepdims=True) * (1.0 / inner)
            total = total + g * lax.rsqrt(power + 1e-05)
    load.wait()
    out[...] = dot((total * small[GAIN_AT : GAIN_AT + 1, :inner]).astype(BF16), w_out[...]).astype(BF16)


def on_device(
    base_ids, complement, embedding, w_gate, w_mix, w_step, step_bias, decay_rate,
    conv_weight, conv_bias, skip_gain, norm_gain, w_out,
):
    length = base_ids.shape[0]
    heads = decay_rate.shape[0]
    depth, inner = w_gate.shape
    head_dim = inner // heads
    width = w_mix.shape[1]
    state = (width - inner) // 2
    members = lax.axis_size("ctx")
    position = lax.axis_index("ctx")
    sizes = dict(heads=heads, head_dim=head_dim, state=state)
    letters = embedding.shape[0]
    codes = letters * 128
    vmem = pl.BlockSpec(memory_space=VMEM)
    hbm = pl.BlockSpec(memory_space=pltpu.HBM)
    params = pltpu.CompilerParams(vmem_limit_bytes=VMEM_LIMIT)
    held = lambda a: pltpu.with_memory_space_constraint(a, VMEM)
    outside = lambda a: pltpu.with_memory_space_constraint(a, pltpu.HBM)
    shape = VMEM

    odd = position % 2 == 1
    across = [(i, (i + 1) % members if i % 2 else (i - 1) % members) for i in range(members)]
    other = lax.ppermute(base_ids, "ctx", across).reshape(1, length)

    given = (
        base_ids, complement, embedding, w_gate, w_mix, w_step.T, step_bias, decay_rate, conv_weight, conv_bias,
        skip_gain, norm_gain,
    )
    own, wide, xt, small = pl.pallas_call(
        functools.partial(tables_kernel, **sizes),
        out_shape=[
            shape((1, length), I32),
            shape((2, 64, width + 2 * inner), BF16),
            shape((2, inner + state, codes), BF16),
            shape((40, 1024), F32),
        ],
        in_specs=[hbm] * len(given),
        out_specs=[vmem] * 4,
        scratch_shapes=[
            VMEM((2 * LETTER_ROWS, depth), F32),
            VMEM(base_ids.shape, I32),
            pltpu.SMEM(complement.shape, I32),
        ]
        + [VMEM(a.shape, a.dtype) for a in given[2:12]]
        + [pltpu.SemaphoreType.DMA((len(given),))],
        compiler_params=params,
        name="tables",
    )(*[outside(a) for a in given])

    two = jnp.where(odd, jnp.concatenate([own, other]), jnp.concatenate([other, own]))
    got = lax.ppermute(two, "ctx", [(i, i ^ 1) for i in range(members)])
    window = jnp.where(odd, jnp.concatenate([got, two]), jnp.concatenate([two, got]))

    def local(strand, *after):
        return pl.pallas_call(
            functools.partial(local_kernel, strand=strand, **sizes),
            out_shape=[
                shape((2, length, inner), F32),
                shape((2, length, inner), BF16),
                shape((2, length, state), BF16),
            ],
            in_specs=[vmem] * (3 + len(after)),
            out_specs=[vmem] * 3,
            compiler_params=params,
            cost_estimate=pl.CostEstimate(flops=4_000_000_000, bytes_accessed=0, transcendentals=0),
            name="local",
        )(*[held(a) for a in (window, wide, small, *after)])

    bit = 4
    ids = window
    strands = []
    while bit < members:
        got = lax.ppermute(ids, "ctx", [(i, i ^ bit ^ 1) for i in range(members)])
        if len(strands) < 2:
            strands.append(local(len(strands), *([] if bit == 4 else [ids])))
        ids = jnp.where(position & bit == 0, jnp.concatenate([ids, got]), jnp.concatenate([got, ids]))
        bit *= 2
    while len(strands) < 2:
        strands.append(local(len(strands)))
    ids = jnp.where(position & 2 == 0, jnp.roll(ids, -1, axis=0), jnp.roll(ids, 1, axis=0))

    (yg0, eg0, reads0), (yg1, eg1, reads1) = strands
    return pl.pallas_call(
        functools.partial(finish_kernel, **sizes),
        out_shape=jax.ShapeDtypeStruct((length, w_out.shape[1]), BF16),
        in_specs=[vmem] * 10 + [hbm],
        out_specs=vmem,
        scratch_shapes=[VMEM(w_out.shape, BF16), pltpu.SemaphoreType.DMA(())],
        compiler_params=params,
        name="finish",
    )(*[held(a) for a in (ids, wide, xt, small, reads0, yg0, eg0, reads1, yg1, eg1)], outside(w_out))


def solution(mesh):
    return jax.shard_map(
        on_device,
        mesh=mesh,
        in_specs=(P(("dp", "ctx")), P(), P(), P(), P(), P(), P(), P(), P(), P(), P(), P(), P()),
        out_specs=P(("dp", "ctx"), None),
        check_vma=False,
    )
```

```python
import functools

import jax
import jax.numpy as jnp
from jax import lax
from jax.experimental import pallas as pl
from jax.experimental.pallas import tpu as pltpu
from jax.sharding import PartitionSpec as P

F32, BF16, I32 = jnp.float32, jnp.bfloat16, jnp.int32
LETTER_ROWS = 8
CHUNK = 128
VMEM = pltpu.VMEM
VMEM_LIMIT = 24 * 1024 * 1024
DECAY_AT, STEP_AT, GAIN_AT = 768, 896, 32


def dot(a, b, contract=((1,), (0,))):
    return lax.dot_general(a, b, (contract, ((), ())), preferred_element_type=F32)


TN = ((0,), (0,))
NT = ((1,), (1,))


def silu(x):
    half = 0.5 * x
    return half + half * jnp.tanh(half)


def split(x):
    high = x.astype(BF16).astype(F32)
    return high, x - high


def iota(shape, dim):
    return lax.broadcasted_iota(I32, shape, dim)


def onehot_rows(row):
    return jnp.where(jnp.broadcast_to(row, (LETTER_ROWS, row.shape[1])) == iota((LETTER_ROWS, row.shape[1]), 0), 1.0, 0.0)


def digits_of(before):
    first = (before * 41) >> 10
    pair = (before * 205) >> 10
    return first, pair - 5 * first, before - 5 * pair


def code_onehot(shape, code_dim):
    code, slot = iota(shape, code_dim), iota(shape, 1 - code_dim) & 31
    before, last = code & 127, code >> 7
    first, second, third = digits_of(before)
    tap = slot >> 3
    digit = jnp.where(tap == 0, first, jnp.where(tap == 1, second, jnp.where(tap == 2, third, last)))
    return jnp.where(digit == (slot & 7), 1.0, 0.0).astype(BF16)


def head_spread(rows, columns, head_dim):
    low = iota((rows, columns), 0) * head_dim
    lane = iota((rows, columns), 1)
    return jnp.where((lane >= low) & (lane < low + head_dim), 1.0, 0.0)


def tables_kernel(
    base_ids_h, comp_h, emb_h, w_gate_h, w_mix_h, w_step_h, step_bias_h, rate_h, conv_w_h, conv_b_h, skip_h,
    norm_gain_h, w_out_h,
    own, wide, xt, small, turn, w_out,
    e16, ids_v, comp, emb, w_gate, w_mix, w_step, step_bias, rate, conv_w, conv_b, skip, gain_v, sems,
    *, heads, head_dim, state,
):
    pairs = [
        (emb_h, emb), (comp_h, comp), (w_mix_h, w_mix), (w_step_h, w_step), (step_bias_h, step_bias), (rate_h, rate),
        (skip_h, skip), (conv_w_h, conv_w), (conv_b_h, conv_b), (w_gate_h, w_gate), (base_ids_h, ids_v),
        (norm_gain_h, gain_v), (w_out_h, w_out),
    ]
    copies = [pltpu.make_async_copy(a, b, sems.at[n]) for n, (a, b) in enumerate(pairs)]
    for copy in copies:
        copy.start()
    letters, inner = emb.shape[0], heads * head_dim
    e16[...] = jnp.zeros_like(e16)
    copies[0].wait()
    copies[1].wait()
    e16[0:letters, :] = emb[...].astype(F32)
    for v in range(letters):
        e16[LETTER_ROWS + v : LETTER_ROWS + v + 1, :] = e16[pl.ds(comp[v], 1), :]
    rows = e16[...].astype(BF16)
    for copy in copies[2:9]:
        copy.wait()
    mix = dot(rows, w_mix[...]).astype(BF16).astype(F32)
    raw = dot(rows, w_step[...], NT) + step_bias[...].reshape(1, heads)
    step = jnp.maximum(raw, 0.0) + jnp.log1p(jnp.exp(-jnp.abs(raw)))
    decay_t = jnp.transpose(-step * rate[...].reshape(1, heads))
    step_t = jnp.transpose(step)
    for strand in range(2):
        at = slice(strand * LETTER_ROWS, (strand + 1) * LETTER_ROWS)
        small[strand * heads : (strand + 1) * heads, DECAY_AT : DECAY_AT + LETTER_ROWS] = decay_t[:, at]
        small[strand * heads : (strand + 1) * heads, STEP_AT : STEP_AT + LETTER_ROWS] = step_t[:, at]
        for v in range(letters):
            small[strand * heads : (strand + 1) * heads, v * 128 : (v + 1) * 128] = jnp.broadcast_to(
                step_t[:, v : v + 1], (heads, 128)
            )
    spread = head_spread(heads, inner, head_dim).astype(BF16)
    steps = [dot(part.astype(BF16), spread) for part in split(step)]
    skip_high, skip_rest = split(skip[...].reshape(1, heads))
    skip_mid, skip_low = split(skip_rest)
    small[2 * heads : 2 * heads + 1, :inner] = sum(dot(part.astype(BF16), spread) for part in (skip_high, skip_mid, skip_low))
    width, codes = conv_w.shape[1], xt.shape[1]
    by_column = code_onehot((64, codes), 1)
    for strand in range(2):
        letter_rows = mix[strand * LETTER_ROWS : (strand + 1) * LETTER_ROWS]
        weighted = [conv_w[k : k + 1, :] * letter_rows for k in range(4)]
        weighted[3] = weighted[3] + conv_b[...].reshape(1, -1)
        high, low = split(jnp.concatenate(weighted, axis=0))
        both = jnp.concatenate([high, low], axis=0)
        wide[strand, :, :width] = both.astype(BF16)
        if strand == 0:
            across = jnp.transpose(both[:, : inner + state]).astype(BF16)
            for low_row in range(0, inner + state, CHUNK):
                part = silu(dot(across[low_row : low_row + CHUNK], by_column))
                xt[low_row : low_row + CHUNK, :] = part.astype(BF16)
    before = iota((128, 128), 0)
    target = jnp.zeros((128, 128), I32)
    for digit, worth in zip(digits_of(before), (25, 5, 1)):
        for v in range(letters):
            target = target + jnp.where(digit == v, comp[v] * worth, 0)
    turn[...] = jnp.where((target == iota((128, 128), 1)) & (before < 125), 1.0, 0.0).astype(BF16)
    copies[9].wait()
    gate = silu(dot(rows, w_gate[...]).astype(BF16).astype(F32))
    gates = split(gate)
    for strand in range(2):
        at = slice(strand * LETTER_ROWS, (strand + 1) * LETTER_ROWS)
        rest = jnp.zeros((3 * LETTER_ROWS, 2 * inner), F32)
        parts = [jnp.concatenate([gates[n][at], steps[n][at]], axis=1) for n in range(2)]
        wide[strand, :, width:] = jnp.concatenate([rest, parts[0], rest, parts[1]], axis=0).astype(BF16)
    for copy in copies[10:]:
        copy.wait()
    own[...] = ids_v[...].reshape(own.shape)
    small[GAIN_AT : GAIN_AT + 1, :inner] = gain_v[...].reshape(1, inner)


def local_kernel(
    window, wide, small, *rest,
    strand, heads, head_dim, state,
):
    yg, eg, reads = rest[-3:]
    length, inner = window.shape[1], heads * head_dim
    blocks = length // CHUNK
    members, position = lax.axis_size("ctx"), lax.axis_index("ctx")
    odd = position % 2 == 1
    here = jnp.where(odd, window[2:3, :], window[1:2, :])
    back = jnp.where(position == 0, -1, jnp.where(odd, window[1:2, :], window[0:1, :]))
    fore = jnp.where(position == members - 1, -1, jnp.where(odd, window[3:4, :], window[2:3, :]))
    place = iota((1, length), 1)
    rows_behind, rows_ahead = [here], [here]
    for k in (1, 2, 3):
        rows_behind.append(jnp.where(place >= k, pltpu.roll(here, k, 1), pltpu.roll(back, k, 1)))
        rows_ahead.append(
            jnp.where(place < length - k, pltpu.roll(here, length - k, 1), pltpu.roll(fore, length - k, 1))
        )
    ahead = jnp.concatenate([onehot_rows(r) for r in rows_behind[::-1]] * 2, axis=0).astype(BF16)
    behind = jnp.concatenate([onehot_rows(r) for r in rows_ahead[::-1]] * 2, axis=0).astype(BF16)
    own = onehot_rows(here)
    upto = jnp.where(iota((length, length), 0) <= iota((length, length), 1), 1.0, 0.0).astype(BF16)
    count = dot(own.astype(BF16), upto)
    before = count - own
    ld = small[strand * heads : (strand + 1) * heads, DECAY_AT : DECAY_AT + LETTER_ROWS]
    skipx = small[2 * heads : 2 * heads + 1, :inner]
    width = inner + 2 * state
    full = sum(ld[:, v : v + 1] * count[v : v + 1, :] for v in range(5))
    less = sum(ld[:, v : v + 1] * before[v : v + 1, :] for v in range(5))
    full_t, less_t = jnp.transpose(full), jnp.transpose(less)
    spread = head_spread(16, inner, head_dim)
    spread = jnp.concatenate([spread, spread], axis=0).astype(BF16)
    enter = (jnp.exp(full), jnp.exp(full[:, length - 1 : length] - less))
    fill = jnp.zeros((4, length), F32)
    enter = [jnp.concatenate([high, fill, low, fill], axis=0).astype(BF16) for high, low in map(split, enter)]
    row, lane = iota((CHUNK, CHUNK), 0), iota((CHUNK, CHUNK), 1)
    lower, upper = row >= lane, row <= lane
    first_half = iota((CHUNK, CHUNK), 1) < head_dim
    span = lambda i: slice(i * CHUNK, (i + 1) * CHUNK)
    gate = dot(ahead, wide[strand, :, width : width + inner], TN)
    stepx = dot(ahead, wide[strand, :, width + inner :], TN)
    values, stepped, scores = [], [], []
    for way, hot in enumerate((ahead, behind)):
        conv = silu(dot(hot, wide[strand, :, :width], TN))
        x = conv[:, :inner]
        keys, read = conv[:, inner : inner + state].astype(BF16), conv[:, inner + state :].astype(BF16)
        reads[way] = read
        values.append(x)
        stepped.append((x * stepx).astype(BF16))
        scores.append(dot(read, keys, NT))
        eg[way] = (
            dot(enter[way], spread, TN) * gate
        ).astype(BF16)
    cut = {}
    for i in range(blocks):
        for j in range(blocks):
            if i >= j:
                s = scores[0][span(i), span(j)]
                cut[0, i, j] = (jnp.where(lower, s, 0.0) if i == j else s).astype(BF16)
            if i <= j:
                s = scores[1][span(i), span(j)]
                cut[1, i, j] = (jnp.where(upper, s, 0.0) if i == j else s).astype(BF16)
    for pair in range(heads // 2):
        columns = slice(pair * 2 * head_dim, (pair + 1) * 2 * head_dim)
        found = []
        for head in (2 * pair, 2 * pair + 1):
            k = head
            decay = {}
            for i in range(blocks):
                for j in range(blocks):
                    if i >= j:
                        down = full_t[span(i), k : k + 1] - full[k : k + 1, span(j)]
                    if i <= j:
                        up = less[k : k + 1, span(j)] - less_t[span(i), k : k + 1]
                    gap = down if i > j else up if i < j else jnp.where(lower, down, up)
                    decay[i, j] = jnp.exp(gap.astype(BF16))
            for way in range(2):
                out = []
                for i in range(blocks):
                    js = range(i + 1) if way == 0 else range(i, blocks)
                    weights = jnp.concatenate([cut[way, i, j] * decay[i, j] for j in js], axis=1)
                    out.append(dot(weights, stepped[way][js[0] * CHUNK : (js[-1] + 1) * CHUNK, columns]))
                found.append(out)
        for way in range(2):
            for i in range(blocks):
                y = jnp.where(first_half, found[way][i], found[2 + way][i])
                y = y + skipx[:, columns] * values[way][span(i), columns]
                yg[way, span(i), columns] = y * gate[span(i), columns]


def finish_kernel(
    ids, wide, xt, small, turn, w_out, reads0, yg0, eg0, reads1, yg1, eg1, comp_h,
    out,
    comp, moved, sem,
    *, heads, head_dim, state,
):
    members, length = ids.shape
    inner = heads * head_dim
    position = lax.axis_index("ctx")
    letters = 5
    load = pltpu.make_async_copy(comp_h, comp, sem)
    load.start()
    every = ids[...]
    lane = iota((members, length), 1)
    block = iota((members, length), 0)
    prev, after = [], []
    up, down = pltpu.roll(every, 1, 0), pltpu.roll(every, members - 1, 0)
    for k in (1, 2, 3):
        inside, outside = pltpu.roll(every, k, 1), pltpu.roll(up, k, 1)
        found = jnp.where(lane >= k, inside, outside)
        prev.append(jnp.where((block == 0) & (lane < k), -1, found))
        inside, outside = pltpu.roll(every, length - k, 1), pltpu.roll(down, length - k, 1)
        found = jnp.where(lane < length - k, inside, outside)
        after.append(jnp.where((block == members - 1) & (lane >= length - k), -1, found))
    code_ahead = jnp.where((block == 0) & (lane < 3), -1, prev[2] * 25 + prev[1] * 5 + prev[0])
    code_behind = jnp.where((block == members - 1) & (lane >= length - 3), -1, after[2] * 25 + after[1] * 5 + after[0])
    code_behind = jnp.where(code_behind < 0, -1, code_behind + 128)
    code = jnp.where(block < position, code_ahead, jnp.where(block > position, code_behind, -1)).astype(BF16)
    code_rows = iota((256, length), 0).astype(BF16)

    marks = [onehot_rows(every[b : b + 1, :]) for b in range(members)]
    mark = jnp.concatenate(marks, axis=0)
    rows = members * LETTER_ROWS
    its_block = iota((rows, 1), 0) >> 3
    i, j = iota((rows, rows), 0), iota((rows, rows), 1)
    bi, bj = i >> 3, j >> 3
    between = ((bi < bj) & (bj < position)) | ((position < bj) & (bj < bi))
    between = jnp.where(((i & 7) == (j & 7)) & between, 1.0, 0.0).astype(BF16)
    amid = dot(between, mark.astype(BF16)).astype(BF16)
    s, t = iota((length, length), 0), iota((length, length), 1)
    later = jnp.where(s > t, 1.0, 0.0).astype(BF16)
    earlier = jnp.where(s < t, 1.0, 0.0).astype(BF16)
    ones = jnp.ones((length, length), BF16)
    counts = (
        dot(jnp.where(its_block < position, mark, 0.0).astype(BF16), later)
        + dot(jnp.where(its_block > position, mark, 0.0).astype(BF16), earlier)
        + dot(amid, ones)
    )
    ld = small[: 2 * heads, DECAY_AT : DECAY_AT + LETTER_ROWS]
    weighed, hot, far = [], [], {}
    for b in range(members):
        count = counts[b * LETTER_ROWS : (b + 1) * LETTER_ROWS]
        far_b = jnp.exp(sum(ld[:, v : v + 1] * count[v : v + 1, :] for v in range(letters)))
        if b in (0, members - 1):
            far[b] = far_b
        weighed.append(jnp.concatenate([far_b * marks[b][v : v + 1, :] for v in range(letters)], axis=0).astype(BF16))
        hot.append(jnp.where(code_rows == code[b : b + 1, :], BF16(1), BF16(0)))
    sums = dot(jnp.concatenate(weighed, axis=1), jnp.concatenate(hot, axis=1), NT)

    edge_lane = iota((1, 128), 1)
    tail = slice(length - 128, length)
    digits = [jnp.where(edge_lane < 64, prev[2 - k][0:1, :128], after[2 - k][members - 1 :, tail]) for k in range(3)]
    digits.append(jnp.where(edge_lane < 64, every[0:1, :128], every[members - 1 :, tail]))
    edge_hot = jnp.concatenate([onehot_rows(d) for d in digits] * 2, axis=0)
    edge_hot = jnp.where((edge_lane < 3) | (edge_lane >= 125), edge_hot, 0.0)
    edge_hot = jnp.concatenate([edge_hot, pltpu.roll(edge_hot, 8, 1)], axis=0).astype(BF16)
    edge = silu(dot(wide[:, :, : inner + state].reshape(128, inner + state), edge_hot, TN)).astype(BF16)
    keys = jnp.concatenate([xt[inner:, :], edge[inner:]], axis=1)
    st = small[: 2 * heads, STEP_AT : STEP_AT + LETTER_ROWS]
    stepk = small[: 2 * heads, : letters * 128]
    first_step = sum(st[:, v : v + 1] * marks[0][v : v + 1, :128] for v in range(letters))
    last_step = sum(st[:, v : v + 1] * marks[members - 1][v : v + 1, tail] for v in range(letters))
    edge_ahead = jnp.where((edge_lane < 3) & (position > 0), far[0][:, :128] * first_step, 0.0)
    edge_behind = jnp.where(
        (edge_lane >= 125) & (position < members - 1), far[members - 1][:, tail] * last_step, 0.0
    )
    span = 2 * heads
    total = jnp.zeros((length, inner), F32)
    weights = []
    load.wait()
    first_strand = iota((span, 1), 0) < heads
    both = jnp.concatenate([sums[:, :128], sums[:, 128:]], axis=0)
    turned = dot(both.astype(BF16), turn[...])
    for way, rim in enumerate((edge_ahead, edge_behind)):
        base = way * letters * span
        by_code = jnp.concatenate([both[base + v * span : base + (v + 1) * span] for v in range(letters)], axis=1)
        for v in range(letters):
            at = pl.multiple_of(comp[v] * 128, 128)
            moved[way, :, pl.ds(at, 128)] = turned[base + v * span : base + (v + 1) * span]
        by_code = jnp.where(first_strand, by_code, moved[way]) * stepk
        rim = jnp.where(first_strand, rim, pltpu.roll(rim, 8, 1))
        weights.append(jnp.concatenate([by_code, rim], axis=1).astype(BF16))
    for strand in range(2):
        for way in range(2):
            scaled = []
            for head in range(heads):
                at = slice(head * head_dim, (head + 1) * head_dim)
                x_head = jnp.concatenate([xt[at, :], edge[at]], axis=1)
                scaled.append(x_head * weights[way][strand * heads + head : strand * heads + head + 1, :])
            entering = dot(keys, jnp.concatenate(scaled, axis=0), NT).astype(BF16)
            reads, yg, eg = ((reads0, yg0, eg0), (reads1, yg1, eg1))[strand]
            carried = dot(reads[way], entering)
            g = yg[way] + carried * eg[way].astype(F32)
            power = jnp.sum(g * g, axis=1, keepdims=True) * (1.0 / inner)
            total = total + g * lax.rsqrt(power + 1e-05)
    out[...] = dot((total * small[GAIN_AT : GAIN_AT + 1, :inner]).astype(BF16), w_out[...]).astype(BF16)


def on_device(
    base_ids, complement, embedding, w_gate, w_mix, w_step, step_bias, decay_rate,
    conv_weight, conv_bias, skip_gain, norm_gain, w_out,
):
    length = base_ids.shape[0]
    heads = decay_rate.shape[0]
    depth, inner = w_gate.shape
    head_dim = inner // heads
    width = w_mix.shape[1]
    state = (width - inner) // 2
    members = lax.axis_size("ctx")
    position = lax.axis_index("ctx")
    sizes = dict(heads=heads, head_dim=head_dim, state=state)
    letters = embedding.shape[0]
    codes = letters * 128
    vmem = pl.BlockSpec(memory_space=VMEM)
    hbm = pl.BlockSpec(memory_space=pltpu.HBM)
    params = pltpu.CompilerParams(vmem_limit_bytes=VMEM_LIMIT)
    held = lambda a: pltpu.with_memory_space_constraint(a, VMEM)
    outside = lambda a: pltpu.with_memory_space_constraint(a, pltpu.HBM)
    shape = VMEM

    odd = position % 2 == 1
    across = [(i, (i + 1) % members if i % 2 else (i - 1) % members) for i in range(members)]
    other = lax.ppermute(base_ids, "ctx", across).reshape(1, length)

    given = (
        base_ids, complement, embedding, w_gate, w_mix, w_step.T, step_bias, decay_rate, conv_weight, conv_bias,
        skip_gain, norm_gain, w_out,
    )
    own, wide, xt, small, turn, w_out_v = pl.pallas_call(
        functools.partial(tables_kernel, **sizes),
        out_shape=[
            shape((1, length), I32),
            shape((2, 64, width + 2 * inner), BF16),
            shape((inner + state, codes), BF16),
            shape((40, 1024), F32),
            shape((128, 128), BF16),
            shape(w_out.shape, BF16),
        ],
        in_specs=[hbm] * len(given),
        out_specs=[vmem] * 6,
        scratch_shapes=[
            VMEM((2 * LETTER_ROWS, depth), F32),
            VMEM(base_ids.shape, I32),
            pltpu.SMEM(complement.shape, I32),
        ]
        + [VMEM(a.shape, a.dtype) for a in given[2:12]]
        + [pltpu.SemaphoreType.DMA((len(given),))],
        compiler_params=params,
        name="tables",
    )(*[outside(a) for a in given])

    two = jnp.where(odd, jnp.concatenate([own, other]), jnp.concatenate([other, own]))
    got = lax.ppermute(two, "ctx", [(i, i ^ 1) for i in range(members)])
    window = jnp.where(odd, jnp.concatenate([got, two]), jnp.concatenate([two, got]))

    def local(strand, *after):
        return pl.pallas_call(
            functools.partial(local_kernel, strand=strand, **sizes),
            out_shape=[
                shape((2, length, inner), F32),
                shape((2, length, inner), BF16),
                shape((2, length, state), BF16),
            ],
            in_specs=[vmem] * (3 + len(after)),
            out_specs=[vmem] * 3,
            compiler_params=params,
            cost_estimate=pl.CostEstimate(flops=4_000_000_000, bytes_accessed=0, transcendentals=0),
            name="local",
        )(*[held(a) for a in (window, wide, small, *after)])

    bit = 4
    ids = window
    strands = []
    while bit < members:
        got = lax.ppermute(ids, "ctx", [(i, i ^ bit ^ 1) for i in range(members)])
        if len(strands) < 2:
            strands.append(local(len(strands), *([] if bit == 4 else [ids])))
        ids = jnp.where(position & bit == 0, jnp.concatenate([ids, got]), jnp.concatenate([got, ids]))
        bit *= 2
    while len(strands) < 2:
        strands.append(local(len(strands)))
    ids = jnp.where(position & 2 == 0, jnp.roll(ids, -1, axis=0), jnp.roll(ids, 1, axis=0))

    (yg0, eg0, reads0), (yg1, eg1, reads1) = strands
    return pl.pallas_call(
        functools.partial(finish_kernel, **sizes),
        out_shape=jax.ShapeDtypeStruct((length, w_out.shape[1]), BF16),
        in_specs=[vmem] * 12 + [hbm],
        out_specs=vmem,
        scratch_shapes=[
            pltpu.SMEM(complement.shape, I32),
            VMEM((2, 2 * heads, codes), F32),
            pltpu.SemaphoreType.DMA(()),
        ],
        compiler_params=params,
        name="finish",
    )(
        *[held(a) for a in (ids, wide, xt, small, turn, w_out_v, reads0, yg0, eg0, reads1, yg1, eg1)],
        outside(complement),
    )


def solution(mesh):
    return jax.shard_map(
        on_device,
        mesh=mesh,
        in_specs=(P(("dp", "ctx")), P(), P(), P(), P(), P(), P(), P(), P(), P(), P(), P(), P()),
        out_specs=P(("dp", "ctx"), None),
        check_vma=False,
    )
```

```python
import functools

import jax
import jax.numpy as jnp
from jax import lax
from jax.experimental import pallas as pl
from jax.experimental.pallas import tpu as pltpu
from jax.sharding import PartitionSpec as P

F32, BF16, I32 = jnp.float32, jnp.bfloat16, jnp.int32
LETTER_ROWS = 8
CHUNK = 128
VMEM = pltpu.VMEM
VMEM_LIMIT = 24 * 1024 * 1024
DECAY_AT, STEP_AT, GAIN_AT = 768, 896, 32


def dot(a, b, contract=((1,), (0,))):
    return lax.dot_general(a, b, (contract, ((), ())), preferred_element_type=F32)


TN = ((0,), (0,))
NT = ((1,), (1,))


def silu(x):
    half = 0.5 * x
    return half + half * jnp.tanh(half)


def split(x):
    high = x.astype(BF16).astype(F32)
    return high, x - high


def iota(shape, dim):
    return lax.broadcasted_iota(I32, shape, dim)


def onehot_rows(row):
    return jnp.where(jnp.broadcast_to(row, (LETTER_ROWS, row.shape[1])) == iota((LETTER_ROWS, row.shape[1]), 0), 1.0, 0.0)


def digits_of(before):
    first = (before * 41) >> 10
    pair = (before * 205) >> 10
    return first, pair - 5 * first, before - 5 * pair


def code_onehot(shape, code_dim):
    code, slot = iota(shape, code_dim), iota(shape, 1 - code_dim) & 31
    before, last = code & 127, code >> 7
    first, second, third = digits_of(before)
    tap = slot >> 3
    digit = jnp.where(tap == 0, first, jnp.where(tap == 1, second, jnp.where(tap == 2, third, last)))
    return jnp.where(digit == (slot & 7), 1.0, 0.0).astype(BF16)


def head_spread(rows, columns, head_dim):
    low = iota((rows, columns), 0) * head_dim
    lane = iota((rows, columns), 1)
    return jnp.where((lane >= low) & (lane < low + head_dim), 1.0, 0.0)


def tables_kernel(
    base_ids_h, comp_h, emb_h, w_gate_h, w_mix_h, w_step_h, step_bias_h, rate_h, conv_w_h, conv_b_h, skip_h,
    norm_gain_h,
    own, wide, small,
    e16, ids_v, comp, emb, w_gate, w_mix, w_step, step_bias, rate, conv_w, conv_b, skip, gain_v, sems,
    *, heads, head_dim, state,
):
    pairs = [
        (emb_h, emb), (comp_h, comp), (w_mix_h, w_mix), (w_step_h, w_step), (step_bias_h, step_bias), (rate_h, rate),
        (skip_h, skip), (conv_w_h, conv_w), (conv_b_h, conv_b), (w_gate_h, w_gate), (base_ids_h, ids_v),
        (norm_gain_h, gain_v),
    ]
    copies = [pltpu.make_async_copy(a, b, sems.at[n]) for n, (a, b) in enumerate(pairs)]
    for copy in copies:
        copy.start()
    letters, inner = emb.shape[0], heads * head_dim
    e16[...] = jnp.zeros_like(e16)
    copies[0].wait()
    copies[1].wait()
    e16[0:letters, :] = emb[...].astype(F32)
    for v in range(letters):
        e16[LETTER_ROWS + v : LETTER_ROWS + v + 1, :] = e16[pl.ds(comp[v], 1), :]
    rows = e16[...].astype(BF16)
    for copy in copies[2:9]:
        copy.wait()
    mix = dot(rows, w_mix[...]).astype(BF16).astype(F32)
    raw = dot(rows, w_step[...], NT) + step_bias[...].reshape(1, heads)
    step = jnp.maximum(raw, 0.0) + jnp.log1p(jnp.exp(-jnp.abs(raw)))
    decay_t = jnp.transpose(-step * rate[...].reshape(1, heads))
    step_t = jnp.transpose(step)
    for strand in range(2):
        at = slice(strand * LETTER_ROWS, (strand + 1) * LETTER_ROWS)
        small[strand * heads : (strand + 1) * heads, DECAY_AT : DECAY_AT + LETTER_ROWS] = decay_t[:, at]
        small[strand * heads : (strand + 1) * heads, STEP_AT : STEP_AT + LETTER_ROWS] = step_t[:, at]
        for v in range(letters):
            small[strand * heads : (strand + 1) * heads, v * 128 : (v + 1) * 128] = jnp.broadcast_to(
                step_t[:, v : v + 1], (heads, 128)
            )
    spread = head_spread(heads, inner, head_dim).astype(BF16)
    steps = [dot(part.astype(BF16), spread) for part in split(step)]
    skip_high, skip_rest = split(skip[...].reshape(1, heads))
    skip_mid, skip_low = split(skip_rest)
    small[2 * heads : 2 * heads + 1, :inner] = sum(dot(part.astype(BF16), spread) for part in (skip_high, skip_mid, skip_low))
    width = conv_w.shape[1]
    for strand in range(2):
        letter_rows = mix[strand * LETTER_ROWS : (strand + 1) * LETTER_ROWS]
        weighted = [conv_w[k : k + 1, :] * letter_rows for k in range(4)]
        weighted[3] = weighted[3] + conv_b[...].reshape(1, -1)
        high, low = split(jnp.concatenate(weighted, axis=0))
        both = jnp.concatenate([high, low], axis=0)
        wide[strand, :, :width] = both.astype(BF16)
    copies[9].wait()
    gate = silu(dot(rows, w_gate[...]).astype(BF16).astype(F32))
    gates = split(gate)
    for strand in range(2):
        at = slice(strand * LETTER_ROWS, (strand + 1) * LETTER_ROWS)
        rest = jnp.zeros((3 * LETTER_ROWS, 2 * inner), F32)
        parts = [jnp.concatenate([gates[n][at], steps[n][at]], axis=1) for n in range(2)]
        wide[strand, :, width:] = jnp.concatenate([rest, parts[0], rest, parts[1]], axis=0).astype(BF16)
    for copy in copies[10:]:
        copy.wait()
    own[...] = ids_v[...].reshape(own.shape)
    small[GAIN_AT : GAIN_AT + 1, :inner] = gain_v[...].reshape(1, inner)


def codes_kernel(
    wide, _, comp_h, w_out_h,
    xt, turn, w_out,
    comp, sems,
):
    load, load_out = pltpu.make_async_copy(comp_h, comp, sems.at[0]), pltpu.make_async_copy(w_out_h, w_out, sems.at[1])
    load.start()
    load_out.start()
    by_column = code_onehot((64, xt.shape[1]), 1)
    across = jnp.transpose(wide[0, :, : xt.shape[0]].astype(F32)).astype(BF16)
    for low_row in range(0, xt.shape[0], CHUNK):
        part = silu(dot(across[low_row : low_row + CHUNK], by_column))
        xt[low_row : low_row + CHUNK, :] = part.astype(BF16)
    load.wait()
    before = iota((128, 128), 0)
    target = jnp.zeros((128, 128), I32)
    for digit, worth in zip(digits_of(before), (25, 5, 1)):
        for v in range(comp.shape[0]):
            target = target + jnp.where(digit == v, comp[v] * worth, 0)
    turn[...] = jnp.where((target == iota((128, 128), 1)) & (before < 125), 1.0, 0.0).astype(BF16)
    load_out.wait()


def survey(every, start, members, position):
    rows, length = every.shape
    lane = iota((rows, length), 1)
    block = (iota((rows, length), 0) + start) & (members - 1)
    prev, after = [], []
    up, down = pltpu.roll(every, 1, 0), pltpu.roll(every, rows - 1, 0)
    for k in (1, 2, 3):
        inside, outside = pltpu.roll(every, k, 1), pltpu.roll(up, k, 1)
        found = jnp.where(lane >= k, inside, outside)
        prev.append(jnp.where((block == 0) & (lane < k), -1, found))
        inside, outside = pltpu.roll(every, length - k, 1), pltpu.roll(down, length - k, 1)
        found = jnp.where(lane < length - k, inside, outside)
        after.append(jnp.where((block == members - 1) & (lane >= length - k), -1, found))
    code_ahead = jnp.where((block == 0) & (lane < 3), -1, prev[2] * 25 + prev[1] * 5 + prev[0])
    code_behind = after[2] * 25 + after[1] * 5 + after[0] + 128
    code_behind = jnp.where((block == members - 1) & (lane >= length - 3), -1, code_behind)
    code = jnp.where(block < position, code_ahead, jnp.where(block > position, code_behind, -1)).astype(BF16)

    mark = jnp.concatenate([onehot_rows(every[b : b + 1, :]) for b in range(rows)], axis=0)
    groups = rows * LETTER_ROWS
    its_block = ((iota((groups, 1), 0) >> 3) + start) & (members - 1)
    i, j = iota((groups, groups), 0), iota((groups, groups), 1)
    bi, bj = ((i >> 3) + start) & (members - 1), ((j >> 3) + start) & (members - 1)
    between = ((bi < bj) & (bj < position)) | ((position < bj) & (bj < bi))
    between = jnp.where(((i & 7) == (j & 7)) & between, 1.0, 0.0).astype(BF16)
    amid = dot(between, mark.astype(BF16)).astype(BF16)
    s, t = iota((length, length), 0), iota((length, length), 1)
    later = jnp.where(s > t, 1.0, 0.0).astype(BF16)
    earlier = jnp.where(s < t, 1.0, 0.0).astype(BF16)
    ones = jnp.ones((length, length), BF16)
    counts = (
        dot(jnp.where(its_block < position, mark, 0.0).astype(BF16), later)
        + dot(jnp.where(its_block > position, mark, 0.0).astype(BF16), earlier)
        + dot(amid, ones)
    )
    return code, mark, counts, prev, after


def decayed(ld, count):
    return jnp.exp(sum(ld[:, v : v + 1] * count[v : v + 1, :] for v in range(5)))


def code_sums(code, mark, counts, ld):
    rows, length = code.shape
    code_rows = iota((256, length), 0).astype(BF16)
    weighed, hot = [], []
    for b in range(rows):
        at = slice(b * LETTER_ROWS, (b + 1) * LETTER_ROWS)
        far = decayed(ld, counts[at])
        weighed.append(jnp.concatenate([far * mark[at][v : v + 1, :] for v in range(5)], axis=0).astype(BF16))
        hot.append(jnp.where(code_rows == code[b : b + 1, :], BF16(1), BF16(0)))
    return dot(jnp.concatenate(weighed, axis=1), jnp.concatenate(hot, axis=1), NT)


def ring_start(position):
    return jnp.where((position & 2) == 0, -1, 1)


def local_kernel(
    window, wide, small, *rest,
    strand, heads, head_dim, state,
):
    if len(rest) == 5:
        near_ids, yg, eg, reads, near = rest
    else:
        yg, eg, reads = rest
    length, inner = window.shape[1], heads * head_dim
    blocks = length // CHUNK
    members, position = lax.axis_size("ctx"), lax.axis_index("ctx")
    odd = position % 2 == 1
    here = jnp.where(odd, window[2:3, :], window[1:2, :])
    back = jnp.where(position == 0, -1, jnp.where(odd, window[1:2, :], window[0:1, :]))
    fore = jnp.where(position == members - 1, -1, jnp.where(odd, window[3:4, :], window[2:3, :]))
    place = iota((1, length), 1)
    rows_behind, rows_ahead = [here], [here]
    for k in (1, 2, 3):
        rows_behind.append(jnp.where(place >= k, pltpu.roll(here, k, 1), pltpu.roll(back, k, 1)))
        rows_ahead.append(
            jnp.where(place < length - k, pltpu.roll(here, length - k, 1), pltpu.roll(fore, length - k, 1))
        )
    ahead = jnp.concatenate([onehot_rows(r) for r in rows_behind[::-1]] * 2, axis=0).astype(BF16)
    behind = jnp.concatenate([onehot_rows(r) for r in rows_ahead[::-1]] * 2, axis=0).astype(BF16)
    own = onehot_rows(here)
    upto = jnp.where(iota((length, length), 0) <= iota((length, length), 1), 1.0, 0.0).astype(BF16)
    count = dot(own.astype(BF16), upto)
    before = count - own
    ld = small[strand * heads : (strand + 1) * heads, DECAY_AT : DECAY_AT + LETTER_ROWS]
    skipx = small[2 * heads : 2 * heads + 1, :inner]
    width = inner + 2 * state
    full = sum(ld[:, v : v + 1] * count[v : v + 1, :] for v in range(5))
    less = sum(ld[:, v : v + 1] * before[v : v + 1, :] for v in range(5))
    full_t, less_t = jnp.transpose(full), jnp.transpose(less)
    spread = head_spread(16, inner, head_dim)
    spread = jnp.concatenate([spread, spread], axis=0).astype(BF16)
    enter = (jnp.exp(full), jnp.exp(full[:, length - 1 : length] - less))
    fill = jnp.zeros((4, length), F32)
    enter = [jnp.concatenate([high, fill, low, fill], axis=0).astype(BF16) for high, low in map(split, enter)]
    row, lane = iota((CHUNK, CHUNK), 0), iota((CHUNK, CHUNK), 1)
    lower, upper = row >= lane, row <= lane
    first_half = iota((CHUNK, CHUNK), 1) < head_dim
    span = lambda i: slice(i * CHUNK, (i + 1) * CHUNK)
    gate = dot(ahead, wide[strand, :, width : width + inner], TN)
    stepx = dot(ahead, wide[strand, :, width + inner :], TN)
    values, stepped, scores = [], [], []
    for way, hot in enumerate((ahead, behind)):
        conv = silu(dot(hot, wide[strand, :, :width], TN))
        x = conv[:, :inner]
        keys, read = conv[:, inner : inner + state].astype(BF16), conv[:, inner + state :].astype(BF16)
        reads[way] = read
        values.append(x)
        stepped.append((x * stepx).astype(BF16))
        scores.append(dot(read, keys, NT))
        eg[way] = (
            dot(enter[way], spread, TN) * gate
        ).astype(BF16)
    cut = {}
    for i in range(blocks):
        for j in range(blocks):
            if i >= j:
                s = scores[0][span(i), span(j)]
                cut[0, i, j] = (jnp.where(lower, s, 0.0) if i == j else s).astype(BF16)
            if i <= j:
                s = scores[1][span(i), span(j)]
                cut[1, i, j] = (jnp.where(upper, s, 0.0) if i == j else s).astype(BF16)
    for pair in range(heads // 2):
        columns = slice(pair * 2 * head_dim, (pair + 1) * 2 * head_dim)
        found = []
        for head in (2 * pair, 2 * pair + 1):
            k = head
            decay = {}
            for i in range(blocks):
                for j in range(blocks):
                    if i >= j:
                        down = full_t[span(i), k : k + 1] - full[k : k + 1, span(j)]
                    if i <= j:
                        up = less[k : k + 1, span(j)] - less_t[span(i), k : k + 1]
                    gap = down if i > j else up if i < j else jnp.where(lower, down, up)
                    decay[i, j] = jnp.exp(gap.astype(BF16))
            for way in range(2):
                out = []
                for i in range(blocks):
                    js = range(i + 1) if way == 0 else range(i, blocks)
                    weights = jnp.concatenate([cut[way, i, j] * decay[i, j] for j in js], axis=1)
                    out.append(dot(weights, stepped[way][js[0] * CHUNK : (js[-1] + 1) * CHUNK, columns]))
                found.append(out)
        for way in range(2):
            for i in range(blocks):
                y = jnp.where(first_half, found[way][i], found[2 + way][i])
                y = y + skipx[:, columns] * values[way][span(i), columns]
                yg[way, span(i), columns] = y * gate[span(i), columns]
    if len(rest) == 5:
        rows = near_ids.shape[0]
        start = (position & (members - rows)) + ring_start(position)
        code, mark, counts, _, _ = survey(near_ids[...], start, members, position)
        inner_rows = slice(LETTER_ROWS, (rows - 1) * LETTER_ROWS)
        every_ld = small[: 2 * heads, DECAY_AT : DECAY_AT + LETTER_ROWS]
        near[...] = code_sums(code[1 : rows - 1], mark[inner_rows], counts[inner_rows], every_ld)


def finish_kernel(
    ids, wide, xt, small, turn, w_out, reads0, yg0, eg0, reads1, yg1, eg1, near, comp_h,
    out,
    comp, moved, sem,
    *, heads, head_dim, state, near_rows,
):
    members, length = ids.shape
    inner = heads * head_dim
    position = lax.axis_index("ctx")
    letters = 5
    load = pltpu.make_async_copy(comp_h, comp, sem)
    load.start()
    every = ids[...]
    start = ring_start(position)
    code, mark, counts, prev, after = survey(every, start, members, position)
    ld = small[: 2 * heads, DECAY_AT : DECAY_AT + LETTER_ROWS]
    low = position & (members - near_rows)
    if members == 2 * near_rows:

        def rest(value, size):
            part = lambda a, b: value[a * size : b * size]
            n, m = near_rows, members
            below = jnp.concatenate([part(0, 1), part(n - 1, n), part(n, m)], axis=0)
            above = jnp.concatenate([part(n, n + 1), part(m - 1, m), part(0, n)], axis=0)
            return jnp.where(low == 0, below, above)

        sums = code_sums(rest(code.astype(F32), 1).astype(BF16), rest(mark, LETTER_ROWS), rest(counts, LETTER_ROWS), ld)
    else:
        row = iota((members, length), 0)
        code = jnp.where((row > low) & (row < low + near_rows - 1), -1.0, code.astype(F32)).astype(BF16)
        sums = code_sums(code, mark, counts, ld)
    sums = sums + near[...]
    even = start < 0

    def end_rows(value, size, last):
        at = (0, members - 2) if last else (1, members - 1)
        return jnp.where(even, *[value[n * size : (n + 1) * size] for n in at])

    edge_lane = iota((1, 128), 1)
    tail = slice(length - 128, length)
    digits = [
        jnp.where(edge_lane < 64, end_rows(before, 1, False)[:, :128], end_rows(behind, 1, True)[:, tail])
        for before, behind in zip(prev[::-1] + [every], after[::-1] + [every])
    ]
    edge_hot = jnp.concatenate([onehot_rows(d) for d in digits] * 2, axis=0)
    edge_hot = jnp.where((edge_lane < 3) | (edge_lane >= 125), edge_hot, 0.0)
    edge_hot = jnp.concatenate([edge_hot, pltpu.roll(edge_hot, 8, 1)], axis=0).astype(BF16)
    edge = silu(dot(wide[:, :, : inner + state].reshape(128, inner + state), edge_hot, TN)).astype(BF16)
    keys = jnp.concatenate([xt[inner:, :], edge[inner:]], axis=1)
    st = small[: 2 * heads, STEP_AT : STEP_AT + LETTER_ROWS]
    stepk = small[: 2 * heads, : letters * 128]
    ends = []
    for last, lanes in ((False, slice(0, 128)), (True, tail)):
        marks = end_rows(mark, LETTER_ROWS, last)[:, lanes]
        step = sum(st[:, v : v + 1] * marks[v : v + 1, :] for v in range(letters))
        ends.append(decayed(ld, end_rows(counts, LETTER_ROWS, last)[:, lanes]) * step)
    edge_ahead = jnp.where((edge_lane < 3) & (position > 0), ends[0], 0.0)
    edge_behind = jnp.where((edge_lane >= 125) & (position < members - 1), ends[1], 0.0)
    span = 2 * heads
    total = jnp.zeros((length, inner), F32)
    weights = []
    load.wait()
    first_strand = iota((span, 1), 0) < heads
    both = jnp.concatenate([sums[:, :128], sums[:, 128:]], axis=0)
    turned = dot(both.astype(BF16), turn[...])
    for way, rim in enumerate((edge_ahead, edge_behind)):
        base = way * letters * span
        by_code = jnp.concatenate([both[base + v * span : base + (v + 1) * span] for v in range(letters)], axis=1)
        for v in range(letters):
            at = pl.multiple_of(comp[v] * 128, 128)
            moved[way, :, pl.ds(at, 128)] = turned[base + v * span : base + (v + 1) * span]
        by_code = jnp.where(first_strand, by_code, moved[way]) * stepk
        rim = jnp.where(first_strand, rim, pltpu.roll(rim, 8, 1))
        weights.append(jnp.concatenate([by_code, rim], axis=1).astype(BF16))
    for strand in range(2):
        for way in range(2):
            scaled = []
            for head in range(heads):
                at = slice(head * head_dim, (head + 1) * head_dim)
                x_head = jnp.concatenate([xt[at, :], edge[at]], axis=1)
                scaled.append(x_head * weights[way][strand * heads + head : strand * heads + head + 1, :])
            entering = dot(keys, jnp.concatenate(scaled, axis=0), NT).astype(BF16)
            reads, yg, eg = ((reads0, yg0, eg0), (reads1, yg1, eg1))[strand]
            carried = dot(reads[way], entering)
            g = yg[way] + carried * eg[way].astype(F32)
            power = jnp.sum(g * g, axis=1, keepdims=True) * (1.0 / inner)
            total = total + g * lax.rsqrt(power + 1e-05)
    out[...] = dot((total * small[GAIN_AT : GAIN_AT + 1, :inner]).astype(BF16), w_out[...]).astype(BF16)


def on_device(
    base_ids, complement, embedding, w_gate, w_mix, w_step, step_bias, decay_rate,
    conv_weight, conv_bias, skip_gain, norm_gain, w_out,
):
    length = base_ids.shape[0]
    heads = decay_rate.shape[0]
    depth, inner = w_gate.shape
    head_dim = inner // heads
    width = w_mix.shape[1]
    state = (width - inner) // 2
    members = lax.axis_size("ctx")
    position = lax.axis_index("ctx")
    sizes = dict(heads=heads, head_dim=head_dim, state=state)
    letters = embedding.shape[0]
    codes = letters * 128
    vmem = pl.BlockSpec(memory_space=VMEM)
    hbm = pl.BlockSpec(memory_space=pltpu.HBM)
    params = pltpu.CompilerParams(vmem_limit_bytes=VMEM_LIMIT)
    held = lambda a: pltpu.with_memory_space_constraint(a, VMEM)
    outside = lambda a: pltpu.with_memory_space_constraint(a, pltpu.HBM)
    shape = VMEM

    odd = position % 2 == 1
    across = [(i, (i + 1) % members if i % 2 else (i - 1) % members) for i in range(members)]
    other = lax.ppermute(base_ids, "ctx", across).reshape(1, length)

    given = (
        base_ids, complement, embedding, w_gate, w_mix, w_step.T, step_bias, decay_rate, conv_weight, conv_bias,
        skip_gain, norm_gain,
    )
    own, wide, small = pl.pallas_call(
        functools.partial(tables_kernel, **sizes),
        out_shape=[
            shape((1, length), I32),
            shape((2, 64, width + 2 * inner), BF16),
            shape((40, 1024), F32),
        ],
        in_specs=[hbm] * len(given),
        out_specs=[vmem] * 3,
        scratch_shapes=[
            VMEM((2 * LETTER_ROWS, depth), F32),
            VMEM(base_ids.shape, I32),
            pltpu.SMEM(complement.shape, I32),
        ]
        + [VMEM(a.shape, a.dtype) for a in given[2:12]]
        + [pltpu.SemaphoreType.DMA((len(given),))],
        compiler_params=params,
        name="tables",
    )(*[outside(a) for a in given])

    two = jnp.where(odd, jnp.concatenate([own, other]), jnp.concatenate([other, own]))
    got = lax.ppermute(two, "ctx", [(i, i ^ 1) for i in range(members)])
    xt, turn, w_out_v = pl.pallas_call(
        codes_kernel,
        out_shape=[shape((inner + state, codes), BF16), shape((128, 128), BF16), shape(w_out.shape, BF16)],
        in_specs=[vmem] * 2 + [hbm] * 2,
        out_specs=[vmem] * 3,
        scratch_shapes=[pltpu.SMEM(complement.shape, I32), pltpu.SemaphoreType.DMA((2,))],
        compiler_params=params,
        cost_estimate=pl.CostEstimate(flops=2_000_000_000, bytes_accessed=0, transcendentals=0),
        name="codes",
    )(held(wide), held(two), outside(complement), outside(w_out))
    window = jnp.where(odd, jnp.concatenate([got, two]), jnp.concatenate([two, got]))

    def local(strand, *after):
        near = [shape((5 * 2 * heads, 256), F32)] * len(after)
        return pl.pallas_call(
            functools.partial(local_kernel, strand=strand, **sizes),
            out_shape=[
                shape((2, length, inner), F32),
                shape((2, length, inner), BF16),
                shape((2, length, state), BF16),
            ]
            + near,
            in_specs=[vmem] * (3 + len(after)),
            out_specs=[vmem] * (3 + len(after)),
            compiler_params=params,
            cost_estimate=pl.CostEstimate(flops=4_000_000_000, bytes_accessed=0, transcendentals=0),
            name="local",
        )(*[held(a) for a in (window, wide, small, *after)])

    bit = 4
    ids = window
    strands = []
    while bit < members:
        got = lax.ppermute(ids, "ctx", [(i, i ^ bit ^ 1) for i in range(members)])
        if len(strands) < 2:
            near_rows = ids.shape[0]
            strands.append(local(len(strands), *([] if bit == 4 else [ids])))
        ids = jnp.where(position & bit == 0, jnp.concatenate([ids, got]), jnp.concatenate([got, ids]))
        bit *= 2
    (yg0, eg0, reads0), (yg1, eg1, reads1, near) = strands
    return pl.pallas_call(
        functools.partial(finish_kernel, near_rows=near_rows, **sizes),
        out_shape=jax.ShapeDtypeStruct((length, w_out.shape[1]), BF16),
        in_specs=[vmem] * 13 + [hbm],
        out_specs=vmem,
        scratch_shapes=[
            pltpu.SMEM(complement.shape, I32),
            VMEM((2, 2 * heads, codes), F32),
            pltpu.SemaphoreType.DMA(()),
        ],
        compiler_params=params,
        name="finish",
    )(
        *[held(a) for a in (ids, wide, xt, small, turn, w_out_v, reads0, yg0, eg0, reads1, yg1, eg1, near)],
        outside(complement),
    )


def solution(mesh):
    return jax.shard_map(
        on_device,
        mesh=mesh,
        in_specs=(P(("dp", "ctx")), P(), P(), P(), P(), P(), P(), P(), P(), P(), P(), P(), P()),
        out_specs=P(("dp", "ctx"), None),
        check_vma=False,
    )
```

```python
import functools

import jax
import jax.numpy as jnp
from jax import lax
from jax.experimental import pallas as pl
from jax.experimental.pallas import tpu as pltpu
from jax.sharding import PartitionSpec as P

F32, BF16, I32 = jnp.float32, jnp.bfloat16, jnp.int32
LETTER_ROWS = 8
CHUNK = 128
VMEM = pltpu.VMEM
VMEM_LIMIT = 24 * 1024 * 1024
DECAY_AT, STEP_AT, GAIN_AT = 768, 896, 32


def dot(a, b, contract=((1,), (0,))):
    return lax.dot_general(a, b, (contract, ((), ())), preferred_element_type=F32)


TN = ((0,), (0,))
NT = ((1,), (1,))


def silu(x):
    half = 0.5 * x
    return half + half * jnp.tanh(half)


def split(x):
    high = x.astype(BF16).astype(F32)
    return high, x - high


def iota(shape, dim):
    return lax.broadcasted_iota(I32, shape, dim)


def onehot_rows(row):
    return jnp.where(jnp.broadcast_to(row, (LETTER_ROWS, row.shape[1])) == iota((LETTER_ROWS, row.shape[1]), 0), 1.0, 0.0)


def digits_of(before):
    first = (before * 41) >> 10
    pair = (before * 205) >> 10
    return first, pair - 5 * first, before - 5 * pair


def code_onehot(shape, code_dim):
    code, slot = iota(shape, code_dim), iota(shape, 1 - code_dim) & 31
    before, last = code & 127, code >> 7
    first, second, third = digits_of(before)
    tap = slot >> 3
    digit = jnp.where(tap == 0, first, jnp.where(tap == 1, second, jnp.where(tap == 2, third, last)))
    return jnp.where(digit == (slot & 7), 1.0, 0.0).astype(BF16)


def head_spread(rows, columns, head_dim):
    low = iota((rows, columns), 0) * head_dim
    lane = iota((rows, columns), 1)
    return jnp.where((lane >= low) & (lane < low + head_dim), 1.0, 0.0)


def tables_kernel(
    base_ids_h, comp_h, emb_h, w_gate_h, w_mix_h, w_step_h, step_bias_h, rate_h, conv_w_h, conv_b_h, skip_h,
    norm_gain_h,
    own, wide, small,
    e16, ids_v, comp, emb, w_gate, w_mix, w_step, step_bias, rate, conv_w, conv_b, skip, gain_v, sems,
    *, heads, head_dim, state,
):
    pairs = [
        (emb_h, emb), (comp_h, comp), (w_mix_h, w_mix), (w_step_h, w_step), (step_bias_h, step_bias), (rate_h, rate),
        (skip_h, skip), (conv_w_h, conv_w), (conv_b_h, conv_b), (w_gate_h, w_gate), (base_ids_h, ids_v),
        (norm_gain_h, gain_v),
    ]
    copies = [pltpu.make_async_copy(a, b, sems.at[n]) for n, (a, b) in enumerate(pairs)]
    for copy in copies:
        copy.start()
    letters, inner = emb.shape[0], heads * head_dim
    e16[...] = jnp.zeros_like(e16)
    copies[0].wait()
    copies[1].wait()
    e16[0:letters, :] = emb[...].astype(F32)
    for v in range(letters):
        e16[LETTER_ROWS + v : LETTER_ROWS + v + 1, :] = e16[pl.ds(comp[v], 1), :]
    rows = e16[...].astype(BF16)
    for copy in copies[2:9]:
        copy.wait()
    mix = dot(rows, w_mix[...]).astype(BF16).astype(F32)
    raw = dot(rows, w_step[...], NT) + step_bias[...].reshape(1, heads)
    step = jnp.maximum(raw, 0.0) + jnp.log1p(jnp.exp(-jnp.abs(raw)))
    decay_t = jnp.transpose(-step * rate[...].reshape(1, heads))
    step_t = jnp.transpose(step)
    for strand in range(2):
        at = slice(strand * LETTER_ROWS, (strand + 1) * LETTER_ROWS)
        small[strand * heads : (strand + 1) * heads, DECAY_AT : DECAY_AT + LETTER_ROWS] = decay_t[:, at]
        small[strand * heads : (strand + 1) * heads, STEP_AT : STEP_AT + LETTER_ROWS] = step_t[:, at]
        for v in range(letters):
            small[strand * heads : (strand + 1) * heads, v * 128 : (v + 1) * 128] = jnp.broadcast_to(
                step_t[:, v : v + 1], (heads, 128)
            )
    spread = head_spread(heads, inner, head_dim).astype(BF16)
    steps = [dot(part.astype(BF16), spread) for part in split(step)]
    skip_high, skip_rest = split(skip[...].reshape(1, heads))
    skip_mid, skip_low = split(skip_rest)
    small[2 * heads : 2 * heads + 1, :inner] = sum(dot(part.astype(BF16), spread) for part in (skip_high, skip_mid, skip_low))
    width = conv_w.shape[1]
    for strand in range(2):
        letter_rows = mix[strand * LETTER_ROWS : (strand + 1) * LETTER_ROWS]
        weighted = [conv_w[k : k + 1, :] * letter_rows for k in range(4)]
        weighted[3] = weighted[3] + conv_b[...].reshape(1, -1)
        high, low = split(jnp.concatenate(weighted, axis=0))
        both = jnp.concatenate([high, low], axis=0)
        wide[strand, :, :width] = both.astype(BF16)
    copies[9].wait()
    gate = silu(dot(rows, w_gate[...]).astype(BF16).astype(F32))
    gates = split(gate)
    for strand in range(2):
        at = slice(strand * LETTER_ROWS, (strand + 1) * LETTER_ROWS)
        rest = jnp.zeros((3 * LETTER_ROWS, 2 * inner), F32)
        parts = [jnp.concatenate([gates[n][at], steps[n][at]], axis=1) for n in range(2)]
        wide[strand, :, width:] = jnp.concatenate([rest, parts[0], rest, parts[1]], axis=0).astype(BF16)
    for copy in copies[10:]:
        copy.wait()
    own[...] = ids_v[...].reshape(own.shape)
    small[GAIN_AT : GAIN_AT + 1, :inner] = gain_v[...].reshape(1, inner)


def codes_kernel(
    wide, _, comp_h, w_out_h,
    xt, turn, w_out,
    comp, sems,
):
    load, load_out = pltpu.make_async_copy(comp_h, comp, sems.at[0]), pltpu.make_async_copy(w_out_h, w_out, sems.at[1])
    load.start()
    load_out.start()
    by_column = code_onehot((64, xt.shape[1]), 1)
    across = jnp.transpose(wide[0, :, : xt.shape[0]].astype(F32)).astype(BF16)
    for low_row in range(0, xt.shape[0], CHUNK):
        part = silu(dot(across[low_row : low_row + CHUNK], by_column))
        xt[low_row : low_row + CHUNK, :] = part.astype(BF16)
    load.wait()
    before = iota((128, 128), 0)
    target = jnp.zeros((128, 128), I32)
    for digit, worth in zip(digits_of(before), (25, 5, 1)):
        for v in range(comp.shape[0]):
            target = target + jnp.where(digit == v, comp[v] * worth, 0)
    turn[...] = jnp.where((target == iota((128, 128), 1)) & (before < 125), 1.0, 0.0).astype(BF16)
    load_out.wait()


def survey(every, start, members, position):
    rows, length = every.shape
    lane = iota((rows, length), 1)
    block = (iota((rows, length), 0) + start) & (members - 1)
    prev, after = [], []
    up, down = pltpu.roll(every, 1, 0), pltpu.roll(every, rows - 1, 0)
    for k in (1, 2, 3):
        inside, outside = pltpu.roll(every, k, 1), pltpu.roll(up, k, 1)
        found = jnp.where(lane >= k, inside, outside)
        prev.append(jnp.where((block == 0) & (lane < k), -1, found))
        inside, outside = pltpu.roll(every, length - k, 1), pltpu.roll(down, length - k, 1)
        found = jnp.where(lane < length - k, inside, outside)
        after.append(jnp.where((block == members - 1) & (lane >= length - k), -1, found))
    code_ahead = jnp.where((block == 0) & (lane < 3), -1, prev[2] * 25 + prev[1] * 5 + prev[0])
    code_behind = after[2] * 25 + after[1] * 5 + after[0] + 128
    code_behind = jnp.where((block == members - 1) & (lane >= length - 3), -1, code_behind)
    code = jnp.where(block < position, code_ahead, jnp.where(block > position, code_behind, -1)).astype(BF16)

    mark = jnp.concatenate([onehot_rows(every[b : b + 1, :]) for b in range(rows)], axis=0)
    groups = rows * LETTER_ROWS
    its_block = ((iota((groups, 1), 0) >> 3) + start) & (members - 1)
    i, j = iota((groups, groups), 0), iota((groups, groups), 1)
    bi, bj = ((i >> 3) + start) & (members - 1), ((j >> 3) + start) & (members - 1)
    between = ((bi < bj) & (bj < position)) | ((position < bj) & (bj < bi))
    between = jnp.where(((i & 7) == (j & 7)) & between, 1.0, 0.0).astype(BF16)
    amid = dot(between, mark.astype(BF16)).astype(BF16)
    s, t = iota((length, length), 0), iota((length, length), 1)
    later = jnp.where(s > t, 1.0, 0.0).astype(BF16)
    earlier = jnp.where(s < t, 1.0, 0.0).astype(BF16)
    ones = jnp.ones((length, length), BF16)
    counts = (
        dot(jnp.where(its_block < position, mark, 0.0).astype(BF16), later)
        + dot(jnp.where(its_block > position, mark, 0.0).astype(BF16), earlier)
        + dot(amid, ones)
    )
    return code, mark, counts, prev, after


def decayed(ld, count):
    return jnp.exp(sum(ld[:, v : v + 1] * count[v : v + 1, :] for v in range(5)))


def code_sums(code, mark, counts, ld):
    rows, length = code.shape
    code_rows = iota((256, length), 0).astype(BF16)
    weighed, hot = [], []
    for b in range(rows):
        at = slice(b * LETTER_ROWS, (b + 1) * LETTER_ROWS)
        far = decayed(ld, counts[at])
        weighed.append(jnp.concatenate([far * mark[at][v : v + 1, :] for v in range(5)], axis=0).astype(BF16))
        hot.append(jnp.where(code_rows == code[b : b + 1, :], BF16(1), BF16(0)))
    return dot(jnp.concatenate(weighed, axis=1), jnp.concatenate(hot, axis=1), NT)


def ring_start(position):
    return jnp.where((position & 2) == 0, -1, 1)


def local_kernel(
    window, wide, small, *rest,
    strand, heads, head_dim, state,
):
    if len(rest) == 5:
        near_ids, yg, eg, reads, near = rest
    else:
        yg, eg, reads = rest
    length, inner = window.shape[1], heads * head_dim
    blocks = length // CHUNK
    members, position = lax.axis_size("ctx"), lax.axis_index("ctx")
    odd = position % 2 == 1
    here = jnp.where(odd, window[2:3, :], window[1:2, :])
    back = jnp.where(position == 0, -1, jnp.where(odd, window[1:2, :], window[0:1, :]))
    fore = jnp.where(position == members - 1, -1, jnp.where(odd, window[3:4, :], window[2:3, :]))
    place = iota((1, length), 1)
    rows_behind, rows_ahead = [here], [here]
    for k in (1, 2, 3):
        rows_behind.append(jnp.where(place >= k, pltpu.roll(here, k, 1), pltpu.roll(back, k, 1)))
        rows_ahead.append(
            jnp.where(place < length - k, pltpu.roll(here, length - k, 1), pltpu.roll(fore, length - k, 1))
        )
    ahead = jnp.concatenate([onehot_rows(r) for r in rows_behind[::-1]] * 2, axis=0).astype(BF16)
    behind = jnp.concatenate([onehot_rows(r) for r in rows_ahead[::-1]] * 2, axis=0).astype(BF16)
    own = onehot_rows(here)
    upto = jnp.where(iota((length, length), 0) <= iota((length, length), 1), 1.0, 0.0).astype(BF16)
    count = dot(own.astype(BF16), upto)
    before = count - own
    ld = small[strand * heads : (strand + 1) * heads, DECAY_AT : DECAY_AT + LETTER_ROWS]
    skipx = small[2 * heads : 2 * heads + 1, :inner]
    width = inner + 2 * state
    full = sum(ld[:, v : v + 1] * count[v : v + 1, :] for v in range(5))
    less = sum(ld[:, v : v + 1] * before[v : v + 1, :] for v in range(5))
    full_t, less_t = jnp.transpose(full), jnp.transpose(less)
    spread = head_spread(16, inner, head_dim)
    spread = jnp.concatenate([spread, spread], axis=0).astype(BF16)
    enter = (jnp.exp(full), jnp.exp(full[:, length - 1 : length] - less))
    fill = jnp.zeros((4, length), F32)
    enter = [jnp.concatenate([high, fill, low, fill], axis=0).astype(BF16) for high, low in map(split, enter)]
    row, lane = iota((CHUNK, CHUNK), 0), iota((CHUNK, CHUNK), 1)
    lower, upper = row >= lane, row <= lane
    first_half = iota((CHUNK, CHUNK), 1) < head_dim
    span = lambda i: slice(i * CHUNK, (i + 1) * CHUNK)
    gate = dot(ahead, wide[strand, :, width : width + inner], TN)
    stepx = dot(ahead, wide[strand, :, width + inner :], TN)
    values, stepped, scores = [], [], []
    for way, hot in enumerate((ahead, behind)):
        conv = silu(dot(hot, wide[strand, :, :width], TN))
        x = conv[:, :inner]
        keys, read = conv[:, inner : inner + state].astype(BF16), conv[:, inner + state :].astype(BF16)
        reads[way] = read
        values.append(x)
        stepped.append((x * stepx).astype(BF16))
        scores.append(dot(read, keys, NT))
        eg[way] = (
            dot(enter[way], spread, TN) * gate
        ).astype(BF16)
    cut = {}
    for i in range(blocks):
        for j in range(blocks):
            if i >= j:
                s = scores[0][span(i), span(j)]
                cut[0, i, j] = (jnp.where(lower, s, 0.0) if i == j else s).astype(BF16)
            if i <= j:
                s = scores[1][span(i), span(j)]
                cut[1, i, j] = (jnp.where(upper, s, 0.0) if i == j else s).astype(BF16)
    for pair in range(heads // 2):
        columns = slice(pair * 2 * head_dim, (pair + 1) * 2 * head_dim)
        found = []
        for head in (2 * pair, 2 * pair + 1):
            k = head
            decay = {}
            for i in range(blocks):
                for j in range(blocks):
                    if i >= j:
                        down = full_t[span(i), k : k + 1] - full[k : k + 1, span(j)]
                    if i <= j:
                        up = less[k : k + 1, span(j)] - less_t[span(i), k : k + 1]
                    gap = down if i > j else up if i < j else jnp.where(lower, down, up)
                    decay[i, j] = jnp.exp(gap.astype(BF16))
            for way in range(2):
                out = []
                for i in range(blocks):
                    js = range(i + 1) if way == 0 else range(i, blocks)
                    weights = jnp.concatenate([cut[way, i, j] * decay[i, j] for j in js], axis=1)
                    out.append(dot(weights, stepped[way][js[0] * CHUNK : (js[-1] + 1) * CHUNK, columns]))
                found.append(out)
        for way in range(2):
            for i in range(blocks):
                y = jnp.where(first_half, found[way][i], found[2 + way][i])
                y = y + skipx[:, columns] * values[way][span(i), columns]
                yg[way, span(i), columns] = y * gate[span(i), columns]
    if len(rest) == 5:
        rows = near_ids.shape[0]
        start = (position & (members - rows)) + ring_start(position)
        code, mark, counts, _, _ = survey(near_ids[...], start, members, position)
        inner_rows = slice(LETTER_ROWS, (rows - 1) * LETTER_ROWS)
        every_ld = small[: 2 * heads, DECAY_AT : DECAY_AT + LETTER_ROWS]
        near[...] = code_sums(code[1 : rows - 1], mark[inner_rows], counts[inner_rows], every_ld)


def finish_kernel(
    ids, wide, xt, small, turn, w_out, reads0, yg0, eg0, reads1, yg1, eg1, near, comp_h,
    out,
    comp, moved, full, sem,
    *, heads, head_dim, state, near_rows,
):
    members, length = ids.shape
    inner = heads * head_dim
    position = lax.axis_index("ctx")
    letters = 5
    load = pltpu.make_async_copy(comp_h, comp, sem)
    load.start()
    every = ids[...]
    start = ring_start(position)
    code, mark, counts, prev, after = survey(every, start, members, position)
    ld = small[: 2 * heads, DECAY_AT : DECAY_AT + LETTER_ROWS]
    low = position & (members - near_rows)
    if members == 2 * near_rows:

        def rest(value, size):
            part = lambda a, b: value[a * size : b * size]
            n, m = near_rows, members
            below = jnp.concatenate([part(0, 1), part(n - 1, n), part(n, m)], axis=0)
            above = jnp.concatenate([part(n, n + 1), part(m - 1, m), part(0, n)], axis=0)
            return jnp.where(low == 0, below, above)

        sums = code_sums(rest(code.astype(F32), 1).astype(BF16), rest(mark, LETTER_ROWS), rest(counts, LETTER_ROWS), ld)
    else:
        row = iota((members, length), 0)
        code = jnp.where((row > low) & (row < low + near_rows - 1), -1.0, code.astype(F32)).astype(BF16)
        sums = code_sums(code, mark, counts, ld)
    sums = sums + near[...]
    even = start < 0

    def end_rows(value, size, last):
        at = (0, members - 2) if last else (1, members - 1)
        return jnp.where(even, *[value[n * size : (n + 1) * size] for n in at])

    edge_lane = iota((1, 128), 1)
    tail = slice(length - 128, length)
    digits = [
        jnp.where(edge_lane < 64, end_rows(before, 1, False)[:, :128], end_rows(behind, 1, True)[:, tail])
        for before, behind in zip(prev[::-1] + [every], after[::-1] + [every])
    ]
    edge_hot = jnp.concatenate([onehot_rows(d) for d in digits] * 2, axis=0)
    edge_hot = jnp.where((edge_lane < 3) | (edge_lane >= 125), edge_hot, 0.0)
    edge_hot = jnp.concatenate([edge_hot, pltpu.roll(edge_hot, 8, 1)], axis=0).astype(BF16)
    edge = silu(dot(wide[:, :, : inner + state].reshape(128, inner + state), edge_hot, TN))
    for tile, shift in enumerate((0, 125, 120, 117)):
        at = slice(tile * 128, (tile + 1) * 128)
        placed = (pltpu.roll(edge, shift, 1) if shift else edge).astype(BF16)
        full[:, at] = jnp.where(iota((1, 128), 1) >= 125, placed, xt[:, at])
    full[:, 512:] = xt[:, 512:]
    keys = full[inner:, :]
    st = small[: 2 * heads, STEP_AT : STEP_AT + LETTER_ROWS]
    stepk = small[: 2 * heads, : letters * 128]
    ends = []
    for last, lanes in ((False, slice(0, 128)), (True, tail)):
        marks = end_rows(mark, LETTER_ROWS, last)[:, lanes]
        step = sum(st[:, v : v + 1] * marks[v : v + 1, :] for v in range(letters))
        ends.append(decayed(ld, end_rows(counts, LETTER_ROWS, last)[:, lanes]) * step)
    edge_ahead = jnp.where((edge_lane < 3) & (position > 0), ends[0], 0.0)
    edge_behind = jnp.where((edge_lane >= 125) & (position < members - 1), ends[1], 0.0)
    span = 2 * heads
    total = jnp.zeros((length, inner), F32)
    weights = []
    load.wait()
    first_strand = iota((span, 1), 0) < heads
    both = jnp.concatenate([sums[:, :128], sums[:, 128:]], axis=0)
    turned = dot(both.astype(BF16), turn[...])
    for way, rim in enumerate((pltpu.roll(edge_ahead, 125, 1), edge_behind)):
        base = way * letters * span
        by_code = jnp.concatenate([both[base + v * span : base + (v + 1) * span] for v in range(letters)], axis=1)
        for v in range(letters):
            at = pl.multiple_of(comp[v] * 128, 128)
            moved[way, :, pl.ds(at, 128)] = turned[base + v * span : base + (v + 1) * span]
        by_code = jnp.where(first_strand, by_code, moved[way]) * stepk
        none = jnp.zeros_like(rim)
        rims = [none] * letters
        rims[1 - way] = jnp.where(first_strand, rim, 0.0)
        rims[3 - way] = jnp.where(first_strand, 0.0, rim)
        weights.append((by_code + jnp.concatenate(rims, axis=1)).astype(BF16))
    for strand in range(2):
        for way in range(2):
            scaled = []
            for head in range(heads):
                at = slice(head * head_dim, (head + 1) * head_dim)
                scaled.append(full[at, :] * weights[way][strand * heads + head : strand * heads + head + 1, :])
            entering = dot(keys, jnp.concatenate(scaled, axis=0), NT).astype(BF16)
            reads, yg, eg = ((reads0, yg0, eg0), (reads1, yg1, eg1))[strand]
            carried = dot(reads[way], entering)
            g = yg[way] + carried * eg[way].astype(F32)
            power = jnp.sum(g * g, axis=1, keepdims=True) * (1.0 / inner)
            total = total + g * lax.rsqrt(power + 1e-05)
    out[...] = dot((total * small[GAIN_AT : GAIN_AT + 1, :inner]).astype(BF16), w_out[...]).astype(BF16)


def on_device(
    base_ids, complement, embedding, w_gate, w_mix, w_step, step_bias, decay_rate,
    conv_weight, conv_bias, skip_gain, norm_gain, w_out,
):
    length = base_ids.shape[0]
    heads = decay_rate.shape[0]
    depth, inner = w_gate.shape
    head_dim = inner // heads
    width = w_mix.shape[1]
    state = (width - inner) // 2
    members = lax.axis_size("ctx")
    position = lax.axis_index("ctx")
    sizes = dict(heads=heads, head_dim=head_dim, state=state)
    letters = embedding.shape[0]
    codes = letters * 128
    vmem = pl.BlockSpec(memory_space=VMEM)
    hbm = pl.BlockSpec(memory_space=pltpu.HBM)
    params = pltpu.CompilerParams(vmem_limit_bytes=VMEM_LIMIT)
    held = lambda a: pltpu.with_memory_space_constraint(a, VMEM)
    outside = lambda a: pltpu.with_memory_space_constraint(a, pltpu.HBM)
    shape = VMEM

    odd = position % 2 == 1
    across = [(i, (i + 1) % members if i % 2 else (i - 1) % members) for i in range(members)]
    other = lax.ppermute(base_ids, "ctx", across).reshape(1, length)

    given = (
        base_ids, complement, embedding, w_gate, w_mix, w_step.T, step_bias, decay_rate, conv_weight, conv_bias,
        skip_gain, norm_gain,
    )
    own, wide, small = pl.pallas_call(
        functools.partial(tables_kernel, **sizes),
        out_shape=[
            shape((1, length), I32),
            shape((2, 64, width + 2 * inner), BF16),
            shape((40, 1024), F32),
        ],
        in_specs=[hbm] * len(given),
        out_specs=[vmem] * 3,
        scratch_shapes=[
            VMEM((2 * LETTER_ROWS, depth), F32),
            VMEM(base_ids.shape, I32),
            pltpu.SMEM(complement.shape, I32),
        ]
        + [VMEM(a.shape, a.dtype) for a in given[2:12]]
        + [pltpu.SemaphoreType.DMA((len(given),))],
        compiler_params=params,
        name="tables",
    )(*[outside(a) for a in given])

    two = jnp.where(odd, jnp.concatenate([own, other]), jnp.concatenate([other, own]))
    got = lax.ppermute(two, "ctx", [(i, i ^ 1) for i in range(members)])
    xt, turn, w_out_v = pl.pallas_call(
        codes_kernel,
        out_shape=[shape((inner + state, codes), BF16), shape((128, 128), BF16), shape(w_out.shape, BF16)],
        in_specs=[vmem] * 2 + [hbm] * 2,
        out_specs=[vmem] * 3,
        scratch_shapes=[pltpu.SMEM(complement.shape, I32), pltpu.SemaphoreType.DMA((2,))],
        compiler_params=params,
        cost_estimate=pl.CostEstimate(flops=2_000_000_000, bytes_accessed=0, transcendentals=0),
        name="codes",
    )(held(wide), held(two), outside(complement), outside(w_out))
    window = jnp.where(odd, jnp.concatenate([got, two]), jnp.concatenate([two, got]))

    def local(strand, *after):
        near = [shape((5 * 2 * heads, 256), F32)] * len(after)
        return pl.pallas_call(
            functools.partial(local_kernel, strand=strand, **sizes),
            out_shape=[
                shape((2, length, inner), F32),
                shape((2, length, inner), BF16),
                shape((2, length, state), BF16),
            ]
            + near,
            in_specs=[vmem] * (3 + len(after)),
            out_specs=[vmem] * (3 + len(after)),
            compiler_params=params,
            cost_estimate=pl.CostEstimate(flops=4_000_000_000, bytes_accessed=0, transcendentals=0),
            name="local",
        )(*[held(a) for a in (window, wide, small, *after)])

    bit = 4
    ids = window
    strands = []
    while bit < members:
        got = lax.ppermute(ids, "ctx", [(i, i ^ bit ^ 1) for i in range(members)])
        if len(strands) < 2:
            near_rows = ids.shape[0]
            strands.append(local(len(strands), *([] if bit == 4 else [ids])))
        ids = jnp.where(position & bit == 0, jnp.concatenate([ids, got]), jnp.concatenate([got, ids]))
        bit *= 2
    (yg0, eg0, reads0), (yg1, eg1, reads1, near) = strands
    return pl.pallas_call(
        functools.partial(finish_kernel, near_rows=near_rows, **sizes),
        out_shape=jax.ShapeDtypeStruct((length, w_out.shape[1]), BF16),
        in_specs=[vmem] * 13 + [hbm],
        out_specs=vmem,
        scratch_shapes=[
            pltpu.SMEM(complement.shape, I32),
            VMEM((2, 2 * heads, codes), F32),
            VMEM((inner + state, codes), BF16),
            pltpu.SemaphoreType.DMA(()),
        ],
        compiler_params=params,
        name="finish",
    )(
        *[held(a) for a in (ids, wide, xt, small, turn, w_out_v, reads0, yg0, eg0, reads1, yg1, eg1, near)],
        outside(complement),
    )


def solution(mesh):
    return jax.shard_map(
        on_device,
        mesh=mesh,
        in_specs=(P(("dp", "ctx")), P(), P(), P(), P(), P(), P(), P(), P(), P(), P(), P(), P()),
        out_specs=P(("dp", "ctx"), None),
        check_vma=False,
    )
```

```python
import functools

import jax
import jax.numpy as jnp
from jax import lax
from jax.experimental import pallas as pl
from jax.experimental.pallas import tpu as pltpu
from jax.sharding import PartitionSpec as P

F32, BF16, I32 = jnp.float32, jnp.bfloat16, jnp.int32
LETTER_ROWS = 8
CHUNK = 128
VMEM = pltpu.VMEM
VMEM_LIMIT = 24 * 1024 * 1024
DECAY_AT, STEP_AT, GAIN_AT = 768, 896, 32


def dot(a, b, contract=((1,), (0,))):
    return lax.dot_general(a, b, (contract, ((), ())), preferred_element_type=F32)


TN = ((0,), (0,))
NT = ((1,), (1,))


def silu(x):
    half = 0.5 * x
    return half + half * jnp.tanh(half)


def split(x):
    high = x.astype(BF16).astype(F32)
    return high, x - high


def iota(shape, dim):
    return lax.broadcasted_iota(I32, shape, dim)


def onehot_rows(row):
    return jnp.where(jnp.broadcast_to(row, (LETTER_ROWS, row.shape[1])) == iota((LETTER_ROWS, row.shape[1]), 0), 1.0, 0.0)


def digits_of(before):
    first = (before * 41) >> 10
    pair = (before * 205) >> 10
    return first, pair - 5 * first, before - 5 * pair


def code_onehot(shape, code_dim):
    code, slot = iota(shape, code_dim), iota(shape, 1 - code_dim) & 31
    before, last = code & 127, code >> 7
    first, second, third = digits_of(before)
    tap = slot >> 3
    digit = jnp.where(tap == 0, first, jnp.where(tap == 1, second, jnp.where(tap == 2, third, last)))
    return jnp.where(digit == (slot & 7), 1.0, 0.0).astype(BF16)


def head_spread(rows, columns, head_dim):
    low = iota((rows, columns), 0) * head_dim
    lane = iota((rows, columns), 1)
    return jnp.where((lane >= low) & (lane < low + head_dim), 1.0, 0.0)


def tables_kernel(
    base_ids_h, comp_h, emb_h, w_gate_h, w_mix_h, w_step_h, step_bias_h, rate_h, conv_w_h, conv_b_h, skip_h,
    norm_gain_h,
    own, wide, small,
    e16, ids_v, comp, emb, w_gate, w_mix, w_step, step_bias, rate, conv_w, conv_b, skip, gain_v, sems,
    *, heads, head_dim, state,
):
    half = emb.shape[1] // 2
    first, rest = pl.ds(0, half), pl.ds(half, half)
    pairs = [
        (emb_h, emb), (comp_h, comp), (w_mix_h.at[first], w_mix.at[first]), (w_step_h, w_step), (step_bias_h, step_bias), (rate_h, rate),
        (skip_h, skip), (conv_w_h, conv_w), (conv_b_h, conv_b), (w_gate_h, w_gate), (base_ids_h, ids_v),
        (norm_gain_h, gain_v),
    ]
    pairs.insert(3, (w_mix_h.at[rest], w_mix.at[rest]))
    copies = [pltpu.make_async_copy(a, b, sems.at[n]) for n, (a, b) in enumerate(pairs)]
    for copy in copies:
        copy.start()
    letters, inner = emb.shape[0], heads * head_dim
    e16[...] = jnp.zeros_like(e16)
    copies[0].wait()
    copies[1].wait()
    e16[0:letters, :] = emb[...].astype(F32)
    for v in range(letters):
        e16[LETTER_ROWS + v : LETTER_ROWS + v + 1, :] = e16[pl.ds(comp[v], 1), :]
    rows = e16[...].astype(BF16)
    copies[2].wait()
    mix = dot(rows[:, :half], w_mix[first, :])
    for copy in copies[3:10]:
        copy.wait()
    mix = (mix + dot(rows[:, half:], w_mix[rest, :])).astype(BF16).astype(F32)
    raw = dot(rows, w_step[...], NT) + step_bias[...].reshape(1, heads)
    step = jnp.maximum(raw, 0.0) + jnp.log1p(jnp.exp(-jnp.abs(raw)))
    decay_t = jnp.transpose(-step * rate[...].reshape(1, heads))
    step_t = jnp.transpose(step)
    for strand in range(2):
        at = slice(strand * LETTER_ROWS, (strand + 1) * LETTER_ROWS)
        small[strand * heads : (strand + 1) * heads, DECAY_AT : DECAY_AT + LETTER_ROWS] = decay_t[:, at]
        small[strand * heads : (strand + 1) * heads, STEP_AT : STEP_AT + LETTER_ROWS] = step_t[:, at]
        for v in range(letters):
            small[strand * heads : (strand + 1) * heads, v * 128 : (v + 1) * 128] = jnp.broadcast_to(
                step_t[:, v : v + 1], (heads, 128)
            )
    spread = head_spread(heads, inner, head_dim).astype(BF16)
    steps = [dot(part.astype(BF16), spread) for part in split(step)]
    skip_high, skip_rest = split(skip[...].reshape(1, heads))
    skip_mid, skip_low = split(skip_rest)
    small[2 * heads : 2 * heads + 1, :inner] = sum(dot(part.astype(BF16), spread) for part in (skip_high, skip_mid, skip_low))
    width = conv_w.shape[1]
    for strand in range(2):
        letter_rows = mix[strand * LETTER_ROWS : (strand + 1) * LETTER_ROWS]
        weighted = [conv_w[k : k + 1, :] * letter_rows for k in range(4)]
        weighted[3] = weighted[3] + conv_b[...].reshape(1, -1)
        high, low = split(jnp.concatenate(weighted, axis=0))
        both = jnp.concatenate([high, low], axis=0)
        wide[strand, :, :width] = both.astype(BF16)
    copies[10].wait()
    gate = silu(dot(rows, w_gate[...]).astype(BF16).astype(F32))
    gates = split(gate)
    for strand in range(2):
        at = slice(strand * LETTER_ROWS, (strand + 1) * LETTER_ROWS)
        blank = jnp.zeros((3 * LETTER_ROWS, 2 * inner), F32)
        parts = [jnp.concatenate([gates[n][at], steps[n][at]], axis=1) for n in range(2)]
        wide[strand, :, width:] = jnp.concatenate([blank, parts[0], blank, parts[1]], axis=0).astype(BF16)
    for copy in copies[11:]:
        copy.wait()
    own[...] = ids_v[...].reshape(own.shape)
    small[GAIN_AT : GAIN_AT + 1, :inner] = gain_v[...].reshape(1, inner)


def codes_kernel(
    wide, _, comp_h, w_out_h,
    xt, turn, w_out,
    comp, sems,
):
    load, load_out = pltpu.make_async_copy(comp_h, comp, sems.at[0]), pltpu.make_async_copy(w_out_h, w_out, sems.at[1])
    load.start()
    load_out.start()
    by_column = code_onehot((64, xt.shape[1]), 1)
    across = jnp.transpose(wide[0, :, : xt.shape[0]].astype(F32)).astype(BF16)
    for low_row in range(0, xt.shape[0], CHUNK):
        part = silu(dot(across[low_row : low_row + CHUNK], by_column))
        xt[low_row : low_row + CHUNK, :] = part.astype(BF16)
    load.wait()
    before = iota((128, 128), 0)
    target = jnp.zeros((128, 128), I32)
    for digit, worth in zip(digits_of(before), (25, 5, 1)):
        for v in range(comp.shape[0]):
            target = target + jnp.where(digit == v, comp[v] * worth, 0)
    turn[...] = jnp.where((target == iota((128, 128), 1)) & (before < 125), 1.0, 0.0).astype(BF16)
    load_out.wait()


def survey(every, start, members, position):
    rows, length = every.shape
    lane = iota((rows, length), 1)
    block = (iota((rows, length), 0) + start) & (members - 1)
    prev, after = [], []
    up, down = pltpu.roll(every, 1, 0), pltpu.roll(every, rows - 1, 0)
    for k in (1, 2, 3):
        inside, outside = pltpu.roll(every, k, 1), pltpu.roll(up, k, 1)
        found = jnp.where(lane >= k, inside, outside)
        prev.append(jnp.where((block == 0) & (lane < k), -1, found))
        inside, outside = pltpu.roll(every, length - k, 1), pltpu.roll(down, length - k, 1)
        found = jnp.where(lane < length - k, inside, outside)
        after.append(jnp.where((block == members - 1) & (lane >= length - k), -1, found))
    code_ahead = jnp.where((block == 0) & (lane < 3), -1, prev[2] * 25 + prev[1] * 5 + prev[0])
    code_behind = after[2] * 25 + after[1] * 5 + after[0] + 128
    code_behind = jnp.where((block == members - 1) & (lane >= length - 3), -1, code_behind)
    code = jnp.where(block < position, code_ahead, jnp.where(block > position, code_behind, -1)).astype(BF16)

    mark = jnp.concatenate([onehot_rows(every[b : b + 1, :]) for b in range(rows)], axis=0)
    groups = rows * LETTER_ROWS
    its_block = ((iota((groups, 1), 0) >> 3) + start) & (members - 1)
    i, j = iota((groups, groups), 0), iota((groups, groups), 1)
    bi, bj = ((i >> 3) + start) & (members - 1), ((j >> 3) + start) & (members - 1)
    between = ((bi < bj) & (bj < position)) | ((position < bj) & (bj < bi))
    between = jnp.where(((i & 7) == (j & 7)) & between, 1.0, 0.0).astype(BF16)
    amid = dot(between, mark.astype(BF16)).astype(BF16)
    s, t = iota((length, length), 0), iota((length, length), 1)
    later = jnp.where(s > t, 1.0, 0.0).astype(BF16)
    earlier = jnp.where(s < t, 1.0, 0.0).astype(BF16)
    ones = jnp.ones((length, length), BF16)
    counts = (
        dot(jnp.where(its_block < position, mark, 0.0).astype(BF16), later)
        + dot(jnp.where(its_block > position, mark, 0.0).astype(BF16), earlier)
        + dot(amid, ones)
    )
    return code, mark, counts, prev, after


def decayed(ld, count):
    return jnp.exp(sum(ld[:, v : v + 1] * count[v : v + 1, :] for v in range(5)))


def code_sums(code, mark, counts, ld):
    rows, length = code.shape
    code_rows = iota((256, length), 0).astype(BF16)
    weighed, hot = [], []
    for b in range(rows):
        at = slice(b * LETTER_ROWS, (b + 1) * LETTER_ROWS)
        far = decayed(ld, counts[at])
        weighed.append(jnp.concatenate([far * mark[at][v : v + 1, :] for v in range(5)], axis=0).astype(BF16))
        hot.append(jnp.where(code_rows == code[b : b + 1, :], BF16(1), BF16(0)))
    return dot(jnp.concatenate(weighed, axis=1), jnp.concatenate(hot, axis=1), NT)


def ring_start(position):
    return jnp.where((position & 2) == 0, -1, 1)


def local_kernel(
    window, wide, small, *rest,
    strand, heads, head_dim, state,
):
    if len(rest) == 5:
        near_ids, yg, eg, reads, near = rest
    else:
        yg, eg, reads = rest
    length, inner = window.shape[1], heads * head_dim
    blocks = length // CHUNK
    members, position = lax.axis_size("ctx"), lax.axis_index("ctx")
    odd = position % 2 == 1
    here = jnp.where(odd, window[2:3, :], window[1:2, :])
    back = jnp.where(position == 0, -1, jnp.where(odd, window[1:2, :], window[0:1, :]))
    fore = jnp.where(position == members - 1, -1, jnp.where(odd, window[3:4, :], window[2:3, :]))
    place = iota((1, length), 1)
    rows_behind, rows_ahead = [here], [here]
    for k in (1, 2, 3):
        rows_behind.append(jnp.where(place >= k, pltpu.roll(here, k, 1), pltpu.roll(back, k, 1)))
        rows_ahead.append(
            jnp.where(place < length - k, pltpu.roll(here, length - k, 1), pltpu.roll(fore, length - k, 1))
        )
    ahead = jnp.concatenate([onehot_rows(r) for r in rows_behind[::-1]] * 2, axis=0).astype(BF16)
    behind = jnp.concatenate([onehot_rows(r) for r in rows_ahead[::-1]] * 2, axis=0).astype(BF16)
    own = onehot_rows(here)
    upto = jnp.where(iota((length, length), 0) <= iota((length, length), 1), 1.0, 0.0).astype(BF16)
    count = dot(own.astype(BF16), upto)
    before = count - own
    ld = small[strand * heads : (strand + 1) * heads, DECAY_AT : DECAY_AT + LETTER_ROWS]
    skipx = small[2 * heads : 2 * heads + 1, :inner]
    width = inner + 2 * state
    full = sum(ld[:, v : v + 1] * count[v : v + 1, :] for v in range(5))
    less = sum(ld[:, v : v + 1] * before[v : v + 1, :] for v in range(5))
    full_t, less_t = jnp.transpose(full), jnp.transpose(less)
    spread = head_spread(16, inner, head_dim)
    spread = jnp.concatenate([spread, spread], axis=0).astype(BF16)
    enter = (jnp.exp(full), jnp.exp(full[:, length - 1 : length] - less))
    fill = jnp.zeros((4, length), F32)
    enter = [jnp.concatenate([high, fill, low, fill], axis=0).astype(BF16) for high, low in map(split, enter)]
    row, lane = iota((CHUNK, CHUNK), 0), iota((CHUNK, CHUNK), 1)
    lower, upper = row >= lane, row <= lane
    first_half = iota((CHUNK, CHUNK), 1) < head_dim
    span = lambda i: slice(i * CHUNK, (i + 1) * CHUNK)
    gate = dot(ahead, wide[strand, :, width : width + inner], TN)
    stepx = dot(ahead, wide[strand, :, width + inner :], TN)
    values, stepped, scores = [], [], []
    for way, hot in enumerate((ahead, behind)):
        conv = silu(dot(hot, wide[strand, :, :width], TN))
        x = conv[:, :inner]
        keys, read = conv[:, inner : inner + state].astype(BF16), conv[:, inner + state :].astype(BF16)
        reads[way] = read
        values.append(x)
        stepped.append((x * stepx).astype(BF16))
        scores.append(dot(read, keys, NT))
        eg[way] = (
            dot(enter[way], spread, TN) * gate
        ).astype(BF16)
    cut = {}
    for i in range(blocks):
        for j in range(blocks):
            if i >= j:
                s = scores[0][span(i), span(j)]
                cut[0, i, j] = (jnp.where(lower, s, 0.0) if i == j else s).astype(BF16)
            if i <= j:
                s = scores[1][span(i), span(j)]
                cut[1, i, j] = (jnp.where(upper, s, 0.0) if i == j else s).astype(BF16)
    for pair in range(heads // 2):
        columns = slice(pair * 2 * head_dim, (pair + 1) * 2 * head_dim)
        found = []
        for head in (2 * pair, 2 * pair + 1):
            k = head
            decay = {}
            for i in range(blocks):
                for j in range(blocks):
                    if i >= j:
                        down = full_t[span(i), k : k + 1] - full[k : k + 1, span(j)]
                    if i <= j:
                        up = less[k : k + 1, span(j)] - less_t[span(i), k : k + 1]
                    gap = down if i > j else up if i < j else jnp.where(lower, down, up)
                    decay[i, j] = jnp.exp(gap.astype(BF16))
            for way in range(2):
                out = []
                for i in range(blocks):
                    js = range(i + 1) if way == 0 else range(i, blocks)
                    weights = jnp.concatenate([cut[way, i, j] * decay[i, j] for j in js], axis=1)
                    out.append(dot(weights, stepped[way][js[0] * CHUNK : (js[-1] + 1) * CHUNK, columns]))
                found.append(out)
        for way in range(2):
            for i in range(blocks):
                y = jnp.where(first_half, found[way][i], found[2 + way][i])
                y = y + skipx[:, columns] * values[way][span(i), columns]
                yg[way, span(i), columns] = y * gate[span(i), columns]
    if len(rest) == 5:
        rows = near_ids.shape[0]
        start = (position & (members - rows)) + ring_start(position)
        code, mark, counts, _, _ = survey(near_ids[...], start, members, position)
        inner_rows = slice(LETTER_ROWS, (rows - 1) * LETTER_ROWS)
        every_ld = small[: 2 * heads, DECAY_AT : DECAY_AT + LETTER_ROWS]
        near[...] = code_sums(code[1 : rows - 1], mark[inner_rows], counts[inner_rows], every_ld)


def finish_kernel(
    ids, wide, xt, small, turn, w_out, reads0, yg0, eg0, reads1, yg1, eg1, near, comp_h,
    out,
    comp, moved, full, sem,
    *, heads, head_dim, state, near_rows,
):
    members, length = ids.shape
    inner = heads * head_dim
    position = lax.axis_index("ctx")
    letters = 5
    load = pltpu.make_async_copy(comp_h, comp, sem)
    load.start()
    every = ids[...]
    start = ring_start(position)
    code, mark, counts, prev, after = survey(every, start, members, position)
    ld = small[: 2 * heads, DECAY_AT : DECAY_AT + LETTER_ROWS]
    low = position & (members - near_rows)
    if members == 2 * near_rows:

        def rest(value, size):
            part = lambda a, b: value[a * size : b * size]
            n, m = near_rows, members
            below = jnp.concatenate([part(0, 1), part(n - 1, n), part(n, m)], axis=0)
            above = jnp.concatenate([part(n, n + 1), part(m - 1, m), part(0, n)], axis=0)
            return jnp.where(low == 0, below, above)

        sums = code_sums(rest(code.astype(F32), 1).astype(BF16), rest(mark, LETTER_ROWS), rest(counts, LETTER_ROWS), ld)
    else:
        row = iota((members, length), 0)
        code = jnp.where((row > low) & (row < low + near_rows - 1), -1.0, code.astype(F32)).astype(BF16)
        sums = code_sums(code, mark, counts, ld)
    sums = sums + near[...]
    even = start < 0

    def end_rows(value, size, last):
        at = (0, members - 2) if last else (1, members - 1)
        return jnp.where(even, *[value[n * size : (n + 1) * size] for n in at])

    edge_lane = iota((1, 128), 1)
    tail = slice(length - 128, length)
    digits = [
        jnp.where(edge_lane < 64, end_rows(before, 1, False)[:, :128], end_rows(behind, 1, True)[:, tail])
        for before, behind in zip(prev[::-1] + [every], after[::-1] + [every])
    ]
    edge_hot = jnp.concatenate([onehot_rows(d) for d in digits] * 2, axis=0)
    edge_hot = jnp.where((edge_lane < 3) | (edge_lane >= 125), edge_hot, 0.0)
    edge_hot = jnp.concatenate([edge_hot, pltpu.roll(edge_hot, 8, 1)], axis=0).astype(BF16)
    edge = silu(dot(wide[:, :, : inner + state].reshape(128, inner + state), edge_hot, TN))
    for tile, shift in enumerate((0, 125, 120, 117)):
        at = slice(tile * 128, (tile + 1) * 128)
        placed = (pltpu.roll(edge, shift, 1) if shift else edge).astype(BF16)
        full[:, at] = jnp.where(iota((1, 128), 1) >= 125, placed, xt[:, at])
    full[:, 512:] = xt[:, 512:]
    keys = full[inner:, :]
    st = small[: 2 * heads, STEP_AT : STEP_AT + LETTER_ROWS]
    stepk = small[: 2 * heads, : letters * 128]
    ends = []
    for last, lanes in ((False, slice(0, 128)), (True, tail)):
        marks = end_rows(mark, LETTER_ROWS, last)[:, lanes]
        step = sum(st[:, v : v + 1] * marks[v : v + 1, :] for v in range(letters))
        ends.append(decayed(ld, end_rows(counts, LETTER_ROWS, last)[:, lanes]) * step)
    edge_ahead = jnp.where((edge_lane < 3) & (position > 0), ends[0], 0.0)
    edge_behind = jnp.where((edge_lane >= 125) & (position < members - 1), ends[1], 0.0)
    span = 2 * heads
    total = jnp.zeros((length, inner), F32)
    weights = []
    load.wait()
    first_strand = iota((span, 1), 0) < heads
    both = jnp.concatenate([sums[:, :128], sums[:, 128:]], axis=0)
    turned = dot(both.astype(BF16), turn[...])
    for way, rim in enumerate((pltpu.roll(edge_ahead, 125, 1), edge_behind)):
        base = way * letters * span
        by_code = jnp.concatenate([both[base + v * span : base + (v + 1) * span] for v in range(letters)], axis=1)
        for v in range(letters):
            at = pl.multiple_of(comp[v] * 128, 128)
            moved[way, :, pl.ds(at, 128)] = turned[base + v * span : base + (v + 1) * span]
        by_code = jnp.where(first_strand, by_code, moved[way]) * stepk
        none = jnp.zeros_like(rim)
        rims = [none] * letters
        rims[1 - way] = jnp.where(first_strand, rim, 0.0)
        rims[3 - way] = jnp.where(first_strand, 0.0, rim)
        weights.append((by_code + jnp.concatenate(rims, axis=1)).astype(BF16))
    for strand in range(2):
        for way in range(2):
            scaled = []
            for head in range(heads):
                at = slice(head * head_dim, (head + 1) * head_dim)
                scaled.append(full[at, :] * weights[way][strand * heads + head : strand * heads + head + 1, :])
            entering = dot(keys, jnp.concatenate(scaled, axis=0), NT).astype(BF16)
            reads, yg, eg = ((reads0, yg0, eg0), (reads1, yg1, eg1))[strand]
            carried = dot(reads[way], entering)
            g = yg[way] + carried * eg[way].astype(F32)
            power = jnp.sum(g * g, axis=1, keepdims=True) * (1.0 / inner)
            total = total + g * lax.rsqrt(power + 1e-05)
    out[...] = dot((total * small[GAIN_AT : GAIN_AT + 1, :inner]).astype(BF16), w_out[...]).astype(BF16)


def on_device(
    base_ids, complement, embedding, w_gate, w_mix, w_step, step_bias, decay_rate,
    conv_weight, conv_bias, skip_gain, norm_gain, w_out,
):
    length = base_ids.shape[0]
    heads = decay_rate.shape[0]
    depth, inner = w_gate.shape
    head_dim = inner // heads
    width = w_mix.shape[1]
    state = (width - inner) // 2
    members = lax.axis_size("ctx")
    position = lax.axis_index("ctx")
    sizes = dict(heads=heads, head_dim=head_dim, state=state)
    letters = embedding.shape[0]
    codes = letters * 128
    vmem = pl.BlockSpec(memory_space=VMEM)
    hbm = pl.BlockSpec(memory_space=pltpu.HBM)
    params = pltpu.CompilerParams(vmem_limit_bytes=VMEM_LIMIT)
    held = lambda a: pltpu.with_memory_space_constraint(a, VMEM)
    outside = lambda a: pltpu.with_memory_space_constraint(a, pltpu.HBM)
    shape = VMEM

    odd = position % 2 == 1
    across = [(i, (i + 1) % members if i % 2 else (i - 1) % members) for i in range(members)]
    other = lax.ppermute(base_ids, "ctx", across).reshape(1, length)

    given = (
        base_ids, complement, embedding, w_gate, w_mix, w_step.T, step_bias, decay_rate, conv_weight, conv_bias,
        skip_gain, norm_gain,
    )
    own, wide, small = pl.pallas_call(
        functools.partial(tables_kernel, **sizes),
        out_shape=[
            shape((1, length), I32),
            shape((2, 64, width + 2 * inner), BF16),
            shape((40, 1024), F32),
        ],
        in_specs=[hbm] * len(given),
        out_specs=[vmem] * 3,
        scratch_shapes=[
            VMEM((2 * LETTER_ROWS, depth), F32),
            VMEM(base_ids.shape, I32),
            pltpu.SMEM(complement.shape, I32),
        ]
        + [VMEM(a.shape, a.dtype) for a in given[2:12]]
        + [pltpu.SemaphoreType.DMA((len(given) + 1,))],
        compiler_params=params,
        name="tables",
    )(*[outside(a) for a in given])

    two = jnp.where(odd, jnp.concatenate([own, other]), jnp.concatenate([other, own]))
    got = lax.ppermute(two, "ctx", [(i, i ^ 1) for i in range(members)])
    xt, turn, w_out_v = pl.pallas_call(
        codes_kernel,
        out_shape=[shape((inner + state, codes), BF16), shape((128, 128), BF16), shape(w_out.shape, BF16)],
        in_specs=[vmem] * 2 + [hbm] * 2,
        out_specs=[vmem] * 3,
        scratch_shapes=[pltpu.SMEM(complement.shape, I32), pltpu.SemaphoreType.DMA((2,))],
        compiler_params=params,
        cost_estimate=pl.CostEstimate(flops=2_000_000_000, bytes_accessed=0, transcendentals=0),
        name="codes",
    )(held(wide), held(two), outside(complement), outside(w_out))
    window = jnp.where(odd, jnp.concatenate([got, two]), jnp.concatenate([two, got]))

    def local(strand, *after):
        near = [shape((5 * 2 * heads, 256), F32)] * len(after)
        return pl.pallas_call(
            functools.partial(local_kernel, strand=strand, **sizes),
            out_shape=[
                shape((2, length, inner), F32),
                shape((2, length, inner), BF16),
                shape((2, length, state), BF16),
            ]
            + near,
            in_specs=[vmem] * (3 + len(after)),
            out_specs=[vmem] * (3 + len(after)),
            compiler_params=params,
            cost_estimate=pl.CostEstimate(flops=4_000_000_000, bytes_accessed=0, transcendentals=0),
            name="local",
        )(*[held(a) for a in (window, wide, small, *after)])

    bit = 4
    ids = window
    strands = []
    while bit < members:
        got = lax.ppermute(ids, "ctx", [(i, i ^ bit ^ 1) for i in range(members)])
        if len(strands) < 2:
            near_rows = ids.shape[0]
            strands.append(local(len(strands), *([] if bit == 4 else [ids])))
        ids = jnp.where(position & bit == 0, jnp.concatenate([ids, got]), jnp.concatenate([got, ids]))
        bit *= 2
    (yg0, eg0, reads0), (yg1, eg1, reads1, near) = strands
    return pl.pallas_call(
        functools.partial(finish_kernel, near_rows=near_rows, **sizes),
        out_shape=jax.ShapeDtypeStruct((length, w_out.shape[1]), BF16),
        in_specs=[vmem] * 13 + [hbm],
        out_specs=vmem,
        scratch_shapes=[
            pltpu.SMEM(complement.shape, I32),
            VMEM((2, 2 * heads, codes), F32),
            VMEM((inner + state, codes), BF16),
            pltpu.SemaphoreType.DMA(()),
        ],
        compiler_params=params,
        name="finish",
    )(
        *[held(a) for a in (ids, wide, xt, small, turn, w_out_v, reads0, yg0, eg0, reads1, yg1, eg1, near)],
        outside(complement),
    )


def solution(mesh):
    return jax.shard_map(
        on_device,
        mesh=mesh,
        in_specs=(P(("dp", "ctx")), P(), P(), P(), P(), P(), P(), P(), P(), P(), P(), P(), P()),
        out_specs=P(("dp", "ctx"), None),
        check_vma=False,
    )
```
